256 devices in a mesh: hid: 16 (over x_lo, z), ffn: 16 (over x_hi, y, core).
Axes of the slice: x: 4 (x_hi: 2, x_lo: 2; x = x_hi * 2 + x_lo), y: 4, z: 8, core: 2. Of those that a mesh axis runs over, the one named last changes fastest.
Arguments:
- tokens: bfloat16 [1024, 8192], P('ffn', 'hid'), may hold values from -128 to 128
- lang_ids: int32 [1024], P('ffn'), may hold values from 0 to 15
- gain_table: float32 [16, 8192], P(None, 'hid'), may hold values from 0.1 to 1.9
- gate_weight: bfloat16 [8192, 28672], P('hid', 'ffn'), may hold values from -0.0625 to 0.0625
- up_weight: bfloat16 [8192, 28672], P('hid', 'ffn'), may hold values from -0.0625 to 0.0625
- down_weight: bfloat16 [28672, 8192], P('ffn', 'hid'), may hold values from -0.03125 to 0.03125
Outputs:
- mixed: bfloat16 [1024, 8192], P('ffn', 'hid')
The draws below stay inside these ranges and needn't reach their ends.
All inputs are finite; a program needn't handle non-finite values.
Results may differ from the reference program's by a relative error of at most 0.012.
Values may be sent and summed in bfloat16 or wider, within the bound.
No kernel may reach another device: no remote copies, remote signals or barrier semaphores. Data moves between devices by JAX's collectives and lax.ppermute only.
A program may use at most 128 MiB of HBM per device.

```python
import math
import jax
import jax.numpy as jnp
from jax import lax

D = 8192
FF = 28672
LANGS = 16
TOKENS = 1024
N_HID = 16


def draw_tokens(key, part):
    key = jax.random.fold_in(key, 7)
    key_base, key_cols, key_rows = jax.random.split(key, 3)
    column_scale = 0.6 * 3.0 ** (jnp.arange(D, dtype=jnp.float32) / D)
    column_scale = column_scale * jnp.exp(jax.random.uniform(key_cols, (D,), jnp.float32, -0.35, 0.35))
    base = jnp.clip(jax.random.normal(key_base, (TOKENS, D), jnp.float32), -5.0, 5.0)
    row_scale = jnp.exp(jax.random.uniform(key_rows, (TOKENS, 1), jnp.float32, 0.0, math.log(10.0)))
    return (base * row_scale * column_scale[None, :]).astype(jnp.bfloat16)


def plant(array, own_key, smallest, largest):
    longest = array.shape.index(max(array.shape))
    spots = []
    for shift in (0, 1):
        where = [jax.random.randint(jax.random.fold_in(own_key, axis), (), 0, length) for axis, length in enumerate(array.shape)]
        where[longest] = (where[longest] + shift) % array.shape[longest]
        spots.append(tuple(where))
    return array.at[spots[0]].set(smallest).at[spots[1]].set(largest)


def steps_of(key, extent, cuts, smallest, high):
    factor_of, own = 1.0, jax.random.fold_in(key, 6)
    for axis_at, blocks in cuts:
        draws = jnp.exp(jax.random.uniform(jax.random.fold_in(own, axis_at), (blocks,), jnp.float32, smallest / len(cuts), high / len(cuts)))
        factor_of = factor_of * jnp.repeat(draws, extent[axis_at] // blocks).reshape([-1 if axis == axis_at else 1 for axis in range(len(extent))])
    return factor_of


def gaussian(own_key, shape, spread, reach, cuts=(), kind=jnp.bfloat16):
    level = steps_of(own_key, shape, cuts, -0.22, 0.18) if cuts else 1.0
    array = jax.random.normal(own_key, shape, jnp.float32) * spread * level
    return jnp.minimum(jnp.maximum(array, -reach), reach).astype(kind)


def setup_inputs(seed: int = 0) -> dict:
    splits = jax.random.split(jax.random.key(seed), 7)
    tokens = draw_tokens(jax.random.fold_in(splits[6], 71), 0)
    lang_ids = plant(jax.random.randint(splits[1], (TOKENS,), 0, LANGS), jax.random.fold_in(splits[1], 1), 0, LANGS - 1).astype(jnp.int32)
    gain_table = jnp.clip(1.0 + 0.18 * jax.random.normal(splits[2], (LANGS, D), jnp.float32), 0.1, 1.9)
    gate_weight = gaussian(splits[3], (D, FF), D ** -0.5, 0.0625, ((0, 16), (1, 16)))
    up_weight = gaussian(splits[4], (D, FF), D ** -0.5, 0.0625, ((0, 16), (1, 16)))
    down_weight = gaussian(splits[5], (FF, D), FF ** -0.5, 0.03125, ((0, 16), (1, 16)))
    return {"tokens": tokens, "lang_ids": lang_ids, "gain_table": gain_table, "gate_weight": gate_weight, "up_weight": up_weight, "down_weight": down_weight}


def reference(tokens, lang_ids, gain_table, gate_weight, up_weight, down_weight):
    values = tokens.astype(jnp.float32)
    inverse_rms = lax.rsqrt(lax.optimization_barrier(jnp.mean(values * values, axis=1)) + 1e-05)
    scaled = (values * gain_table[lang_ids]).astype(jnp.bfloat16)
    block_width = D // N_HID
    blocks_in = scaled.reshape(TOKENS, N_HID, block_width).transpose(1, 0, 2)
    both_weights = jnp.concatenate([gate_weight, up_weight], axis=1)
    blocks_weight = both_weights.reshape(N_HID, block_width, 2 * FF)

    def accumulate(total, pair):
        partial_term = jnp.dot(pair[0], pair[1], preferred_element_type=jnp.float32).astype(jnp.bfloat16)
        partial_term = lax.optimization_barrier(partial_term)
        return (total + partial_term.astype(jnp.float32), None)
    summed, _ = lax.scan(accumulate, jnp.zeros((TOKENS, 2 * FF), jnp.float32), (blocks_in, blocks_weight))
    gate_sum = summed[:, :FF] * inverse_rms[:, None]
    up_sum = summed[:, FF:] * inverse_rms[:, None]
    hidden = (jax.nn.silu(gate_sum) * up_sum).astype(jnp.bfloat16)
    projected = jnp.dot(hidden, down_weight, preferred_element_type=jnp.float32)
    return (values + projected).astype(jnp.bfloat16)
```

```python
import jax
import jax.numpy as jnp
from jax import lax
from jax.sharding import PartitionSpec as P

AXES = ("hid", "ffn")
BF = jnp.bfloat16
F32 = jnp.float32


def permutation(move):
    pairs = []
    for xl in range(2):
        for z in range(8):
            for xh in range(2):
                for y in range(4):
                    for core in range(2):
                        x, yy, zz, cc = move(xh * 2 + xl, y, z, core)
                        source = (xl * 8 + z) * 16 + xh * 8 + y * 2 + core
                        target = ((x % 2) * 8 + zz) * 16 + (x // 2) * 8 + yy * 2 + cc
                        pairs.append((source, target))
    return pairs


def swap_x(value, bits):
    return lax.ppermute(value, AXES, permutation(lambda x, y, z, c: (x ^ bits, y, z, c)))


def swap_y(value, bits):
    return lax.ppermute(value, AXES, permutation(lambda x, y, z, c: (x, y ^ bits, z, c)))


def swap_core(value):
    return lax.ppermute(value, AXES, permutation(lambda x, y, z, c: (x, y, z, c ^ 1)))


def shift_z(value, step):
    return lax.ppermute(value, AXES, permutation(lambda x, y, z, c: (x, y, (z + step) % 8, c)))


def add(*terms):
    total = terms[0].astype(F32)
    for term in terms[1:]:
        total = total + term.astype(F32)
    return total


def high_low(value):
    high = value.astype(BF)
    low = (value - high.astype(F32)).astype(BF)
    return high, low


def local(tokens, lang_ids, gain_table, gate_weight, up_weight, down_weight):
    rows, width = tokens.shape
    units = gate_weight.shape[1]
    half = units // 2
    part_a = 512
    part_b = half - part_a
    hid = lax.axis_index("hid")
    x_lo, z = hid // 8, hid % 8

    def columns(weight, start, count):
        return lax.dynamic_slice(weight, (0, start), (weight.shape[0], count))

    def both(start, count):
        return jnp.concatenate(
            [columns(gate_weight, start, count), columns(up_weight, start, count)], axis=1
        )

    other = (1 - x_lo) * half
    own = x_lo * half
    there_a = swap_x(both(other, part_a), 1)
    there_b = swap_x(both(other + part_a, part_b), 1)

    one_hot = (
        lang_ids[:, None] == jnp.arange(gain_table.shape[0], dtype=jnp.int32)[None, :]
    ).astype(F32)
    token_gains = jnp.dot(one_hot, gain_table, precision=lax.Precision.HIGHEST)
    values = tokens.astype(F32)
    scaled = (values * token_gains).astype(BF)
    squares = jnp.sum(values * values, axis=1, keepdims=True)
    high, low = high_low(squares)
    pad = jnp.zeros((rows, 126), BF)
    block = jnp.concatenate([scaled, high, low, pad], axis=1)
    block = lax.dynamic_slice(
        jnp.concatenate([block, block], axis=0), (z * 8, 0), block.shape
    ).reshape(8, 8, width + 128)

    from_1, from_2, from_3 = (swap_x(block, bits) for bits in (1, 2, 3))
    block = jnp.concatenate(
        [
            jnp.concatenate([block, from_2], axis=1),
            jnp.concatenate([from_1, from_3], axis=1),
        ],
        axis=2,
    )
    block = jnp.concatenate([block] + [swap_y(block, bits) for bits in (1, 2, 3)], axis=1)
    block = jnp.concatenate([block, swap_core(block)], axis=1)
    edge = width + 128
    here = block[:, :, :width].reshape(-1, width)
    there = block[:, :, edge : edge + width].reshape(-1, width)
    everything = jnp.concatenate([here, there], axis=1)
    square_sums = add(
        block[:, :, width],
        block[:, :, width + 1],
        block[:, :, edge + width],
        block[:, :, edge + width + 1],
    )

    weight_a = jnp.concatenate([both(own, part_a), there_a], axis=0)
    sums_a = (
        jnp.dot(everything, weight_a, preferred_element_type=F32)
        .astype(BF)
        .reshape(8, -1, 2 * part_a)
    )
    weight_b = jnp.concatenate([both(own + part_a, part_b), there_b], axis=0)
    sums_b = (
        jnp.dot(everything, weight_b, preferred_element_type=F32)
        .astype(BF)
        .reshape(8, -1, 2 * part_b)
    )

    def with_squares(k, arrived=None):
        total = square_sums[k][:, None]
        if arrived is None:
            body = sums_b[k]
        else:
            body = add(sums_b[k], arrived[:, : 2 * part_b]).astype(BF)
            total = total + add(
                arrived[:, 2 * part_b : 2 * part_b + 1],
                arrived[:, 2 * part_b + 1 : 2 * part_b + 2],
            )
        high, low = high_low(total)
        return jnp.concatenate([body, high, low, jnp.zeros((body.shape[0], 126), BF)], axis=1)

    up_a = shift_z(sums_a[4], 1)
    down_a = shift_z(sums_a[5], -1)
    down_b = shift_z(with_squares(4), -1)
    up_b = shift_z(with_squares(3), 1)
    up_a = shift_z(add(sums_a[3], up_a).astype(BF), 1)
    down_a = shift_z(add(sums_a[6], down_a).astype(BF), -1)
    down_b = shift_z(with_squares(5, down_b), -1)
    up_b = shift_z(with_squares(2, up_b), 1)
    up_a = shift_z(add(sums_a[2], up_a).astype(BF), 1)
    down_a = shift_z(add(sums_a[7], down_a).astype(BF), -1)
    down_b = shift_z(with_squares(6, down_b), -1)
    up_b = shift_z(with_squares(1, up_b), 1)
    up_a = shift_z(add(sums_a[1], up_a).astype(BF), 1)
    down_b = shift_z(with_squares(7, down_b), -1)

    cut = 2 * part_b
    all_squares = square_sums[0][:, None] + add(
        up_b[:, cut : cut + 1],
        up_b[:, cut + 1 : cut + 2],
        down_b[:, cut : cut + 1],
        down_b[:, cut + 1 : cut + 2],
    )
    inverse_rms = lax.rsqrt(all_squares / (width * 16) + 1e-05)

    def activate(summed, count):
        gate = summed[:, :count] * inverse_rms
        up = summed[:, count:] * inverse_rms
        return (jax.nn.silu(gate) * up).astype(BF)

    hidden_a = activate(add(sums_a[0], up_a, down_a), part_a)
    hidden_b = activate(add(sums_b[0], up_b[:, :cut], down_b[:, :cut]), part_b)

    chunks = {0: (hidden_a, hidden_b)}
    up, down = chunks[0], chunks[0]
    for step in (1, 2, 3):
        up = (shift_z(up[0], 1), shift_z(up[1], 1))
        down = (shift_z(down[0], -1), shift_z(down[1], -1))
        chunks[8 - step] = up
        chunks[step] = down
    chunks[4] = (shift_z(up[0], 1), shift_z(down[1], -1))

    down_there = swap_x(
        lax.dynamic_slice(down_weight, (other, 0), (half, width)), 1
    )
    down_here = lax.dynamic_slice(down_weight, (own, 0), (half, width))
    down_both = jnp.concatenate([down_here, down_there], axis=1)
    hidden = jnp.concatenate(
        [jnp.concatenate(chunks[k], axis=1) for k in range(8)], axis=0
    )
    terms = (
        jnp.dot(hidden, down_both, preferred_element_type=F32)
        .astype(BF)
        .reshape(8, 128, 2 * width)
    )
    terms = add(terms[:, :64], swap_core(terms[:, 64:])).astype(BF)
    terms = add(
        terms[:, :16],
        swap_y(terms[:, 16:32], 1),
        swap_y(terms[:, 32:48], 2),
        swap_y(terms[:, 48:64], 3),
    ).astype(BF)
    own_rows = add(
        terms[:, :8, :width],
        swap_x(terms[:, :8, width:], 1),
        swap_x(terms[:, 8:, :width], 2),
        swap_x(terms[:, 8:, width:], 3),
    ).reshape(rows, width)
    own_rows = lax.dynamic_slice(
        jnp.concatenate([own_rows, own_rows], axis=0), ((8 - z) % 8 * 8, 0), (rows, width)
    )
    return (values + own_rows).astype(BF)


def solution(mesh):
    return jax.shard_map(
        local,
        mesh=mesh,
        in_specs=(
            P("ffn", "hid"),
            P("ffn"),
            P(None, "hid"),
            P("hid", "ffn"),
            P("hid", "ffn"),
            P("ffn", "hid"),
        ),
        out_specs=P("ffn", "hid"),
        check_vma=False,
    )
```

```python
import jax
import jax.numpy as jnp
from jax import lax
from jax.sharding import PartitionSpec as P

AXES = ("hid", "ffn")
BF = jnp.bfloat16
F32 = jnp.float32


def permutation(move):
    pairs = []
    for xl in range(2):
        for z in range(8):
            for xh in range(2):
                for y in range(4):
                    for core in range(2):
                        x, yy, zz, cc = move(xh * 2 + xl, y, z, core)
                        source = (xl * 8 + z) * 16 + xh * 8 + y * 2 + core
                        target = ((x % 2) * 8 + zz) * 16 + (x // 2) * 8 + yy * 2 + cc
                        pairs.append((source, target))
    return pairs


def swap_x(value, bits):
    return lax.ppermute(value, AXES, permutation(lambda x, y, z, c: (x ^ bits, y, z, c)))


def swap_y(value, bits):
    return lax.ppermute(value, AXES, permutation(lambda x, y, z, c: (x, y ^ bits, z, c)))


def swap_core(value):
    return lax.ppermute(value, AXES, permutation(lambda x, y, z, c: (x, y, z, c ^ 1)))


def shift_z(value, step):
    return lax.ppermute(value, AXES, permutation(lambda x, y, z, c: (x, y, (z + step) % 8, c)))


def tie(*values):
    return lax.optimization_barrier(values)


def add(*terms):
    total = terms[0].astype(F32)
    for term in terms[1:]:
        total = total + term.astype(F32)
    return total


def high_low(value):
    high = value.astype(BF)
    low = (value - high.astype(F32)).astype(BF)
    return high, low


def local(tokens, lang_ids, gain_table, gate_weight, up_weight, down_weight):
    rows, width = tokens.shape
    units = gate_weight.shape[1]
    half = units // 2
    part_a = 512
    part_b = half - part_a
    hid = lax.axis_index("hid")
    x_lo, z = hid // 8, hid % 8

    def columns(weight, start, count):
        return lax.dynamic_slice(weight, (0, start), (weight.shape[0], count))

    def both(start, count):
        return jnp.concatenate(
            [columns(gate_weight, start, count), columns(up_weight, start, count)], axis=1
        )

    other = (1 - x_lo) * half
    own = x_lo * half
    away_a = both(other, part_a)
    away_b = both(other + part_a, part_b)

    one_hot = (
        lang_ids[:, None] == jnp.arange(gain_table.shape[0], dtype=jnp.int32)[None, :]
    ).astype(F32)
    token_gains = jnp.dot(one_hot, gain_table, precision=lax.Precision.HIGHEST)
    values = tokens.astype(F32)
    scaled = (values * token_gains).astype(BF)
    squares = jnp.sum(values * values, axis=1, keepdims=True)
    high, low = high_low(squares)
    pad = jnp.zeros((rows, 126), BF)
    block = jnp.concatenate([scaled, high, low, pad], axis=1)
    block = lax.dynamic_slice(
        jnp.concatenate([block, block], axis=0), (z * 8, 0), block.shape
    ).reshape(8, 8, width + 128)

    block, away_a, away_b = tie(block, away_a, away_b)
    piece_1 = swap_x(away_a[:192], 1)
    from_1, from_2, from_3 = (swap_x(block, bits) for bits in (1, 2, 3))
    from_1, from_2, from_3, piece_1 = tie(from_1, from_2, from_3, piece_1)
    block = jnp.concatenate(
        [
            jnp.concatenate([block, from_2], axis=1),
            jnp.concatenate([from_1, from_3], axis=1),
        ],
        axis=2,
    )
    block, rest_a, first_b = tie(block, away_a[192:], away_b[:192])
    piece_2 = swap_x(rest_a, 1)
    piece_3 = swap_x(first_b, 1)
    from_1, from_2, from_3 = (swap_y(block, bits) for bits in (1, 2, 3))
    from_1, from_2, from_3, piece_2, piece_3, away_b = tie(
        from_1, from_2, from_3, piece_2, piece_3, away_b
    )
    block = jnp.concatenate([block, from_1, from_2, from_3], axis=1)
    piece_4 = swap_x(away_b[192:384], 1)
    from_core = swap_core(block)
    from_core, piece_4, rest_b = tie(from_core, piece_4, away_b[384:])
    piece_5 = swap_x(rest_b, 1)
    block = jnp.concatenate([block, from_core], axis=1)
    edge = width + 128
    here = block[:, :, :width].reshape(-1, width)
    there = block[:, :, edge : edge + width].reshape(-1, width)
    everything = jnp.concatenate([here, there], axis=1)
    square_sums = add(
        block[:, :, width],
        block[:, :, width + 1],
        block[:, :, edge + width],
        block[:, :, edge + width + 1],
    )

    weight_a = jnp.concatenate([both(own, part_a), piece_1, piece_2], axis=0)
    sums_a = (
        jnp.dot(everything, weight_a, preferred_element_type=F32)
        .astype(BF)
        .reshape(8, -1, 2 * part_a)
    )
    weight_b = jnp.concatenate([both(own + part_a, part_b), piece_3, piece_4, piece_5], axis=0)
    sums_b = (
        jnp.dot(everything, weight_b, preferred_element_type=F32)
        .astype(BF)
        .reshape(8, -1, 2 * part_b)
    )

    def with_squares(k, arrived=None):
        total = square_sums[k][:, None]
        if arrived is None:
            body = sums_b[k]
        else:
            body = add(sums_b[k], arrived[:, : 2 * part_b]).astype(BF)
            total = total + add(
                arrived[:, 2 * part_b : 2 * part_b + 1],
                arrived[:, 2 * part_b + 1 : 2 * part_b + 2],
            )
        high, low = high_low(total)
        return jnp.concatenate([body, high, low, jnp.zeros((body.shape[0], 126), BF)], axis=1)

    up_a = shift_z(sums_a[4], 1)
    down_b = shift_z(with_squares(4), -1)
    down_a = up_b = None
    for hop in (1, 2, 3):
        send_up = add(sums_a[4 - hop], up_a).astype(BF)
        send_down = sums_a[5] if down_a is None else add(sums_a[4 + hop], down_a).astype(BF)
        send_up, send_down = tie(send_up, send_down)
        up_a, down_a = shift_z(send_up, 1), shift_z(send_down, -1)
        up_a, down_a = tie(up_a, down_a)
        send_up = with_squares(4 - hop, up_b)
        send_down = with_squares(4 + hop, down_b)
        send_up, send_down = tie(send_up, send_down)
        up_b, down_b = shift_z(send_up, 1), shift_z(send_down, -1)
        up_b, down_b = tie(up_b, down_b)

    cut = 2 * part_b
    all_squares = square_sums[0][:, None] + add(
        up_b[:, cut : cut + 1],
        up_b[:, cut + 1 : cut + 2],
        down_b[:, cut : cut + 1],
        down_b[:, cut + 1 : cut + 2],
    )
    inverse_rms = lax.rsqrt(all_squares / (width * 16) + 1e-05)

    def activate(summed, count):
        gate = summed[:, :count] * inverse_rms
        up = summed[:, count:] * inverse_rms
        return (jax.nn.silu(gate) * up).astype(BF)

    hidden_a = activate(add(sums_a[0], up_a, down_a), part_a)
    hidden_b = activate(add(sums_b[0], up_b[:, :cut], down_b[:, :cut]), part_b)

    chunks = {0: (hidden_a, hidden_b)}
    up, down = chunks[0], chunks[0]
    for step in (1, 2, 3):
        up = (shift_z(up[0], 1), shift_z(up[1], 1))
        down = (shift_z(down[0], -1), shift_z(down[1], -1))
        chunks[8 - step] = up
        chunks[step] = down
    chunks[4] = (shift_z(up[0], 1), shift_z(down[1], -1))

    down_there = swap_x(
        lax.dynamic_slice(down_weight, (other, 0), (half, width)), 1
    )
    down_here = lax.dynamic_slice(down_weight, (own, 0), (half, width))
    down_both = jnp.concatenate([down_here, down_there], axis=1)
    hidden = jnp.concatenate(
        [jnp.concatenate(chunks[k], axis=1) for k in range(8)], axis=0
    )
    terms = (
        jnp.dot(hidden, down_both, preferred_element_type=F32)
        .astype(BF)
        .reshape(8, 128, 2 * width)
    )
    terms = add(terms[:, :64], swap_core(terms[:, 64:])).astype(BF)
    terms = add(
        terms[:, :16],
        swap_y(terms[:, 16:32], 1),
        swap_y(terms[:, 32:48], 2),
        swap_y(terms[:, 48:64], 3),
    ).astype(BF)
    own_rows = add(
        terms[:, :8, :width],
        swap_x(terms[:, :8, width:], 1),
        swap_x(terms[:, 8:, :width], 2),
        swap_x(terms[:, 8:, width:], 3),
    ).reshape(rows, width)
    own_rows = lax.dynamic_slice(
        jnp.concatenate([own_rows, own_rows], axis=0), ((8 - z) % 8 * 8, 0), (rows, width)
    )
    return (values + own_rows).astype(BF)


def solution(mesh):
    return jax.shard_map(
        local,
        mesh=mesh,
        in_specs=(
            P("ffn", "hid"),
            P("ffn"),
            P(None, "hid"),
            P("hid", "ffn"),
            P("hid", "ffn"),
            P("ffn", "hid"),
        ),
        out_specs=P("ffn", "hid"),
        check_vma=False,
    )
```

```python
import jax
import jax.numpy as jnp
from jax import lax
from jax.sharding import PartitionSpec as P

AXES = ("hid", "ffn")
BF = jnp.bfloat16
F32 = jnp.float32


def permutation(move):
    pairs = []
    for xl in range(2):
        for z in range(8):
            for xh in range(2):
                for y in range(4):
                    for core in range(2):
                        x, yy, zz, cc = move(xh * 2 + xl, y, z, core)
                        source = (xl * 8 + z) * 16 + xh * 8 + y * 2 + core
                        target = ((x % 2) * 8 + zz) * 16 + (x // 2) * 8 + yy * 2 + cc
                        pairs.append((source, target))
    return pairs


def swap_x(value, bits):
    return lax.ppermute(value, AXES, permutation(lambda x, y, z, c: (x ^ bits, y, z, c)))


def swap_y(value, bits):
    return lax.ppermute(value, AXES, permutation(lambda x, y, z, c: (x, y ^ bits, z, c)))


def swap_core(value):
    return lax.ppermute(value, AXES, permutation(lambda x, y, z, c: (x, y, z, c ^ 1)))


def shift_z(value, step):
    return lax.ppermute(value, AXES, permutation(lambda x, y, z, c: (x, y, (z + step) % 8, c)))


def tie(*values):
    return lax.optimization_barrier(values)


def add(*terms):
    total = terms[0].astype(F32)
    for term in terms[1:]:
        total = total + term.astype(F32)
    return total


def high_low(value):
    high = value.astype(BF)
    low = (value - high.astype(F32)).astype(BF)
    return high, low


def local(tokens, lang_ids, gain_table, gate_weight, up_weight, down_weight):
    rows, width = tokens.shape
    units = gate_weight.shape[1]
    half = units // 2
    part_a = half - 512
    part_b = half - part_a
    hid = lax.axis_index("hid")
    x_lo, z = hid // 8, hid % 8

    def columns(weight, start, count):
        return lax.dynamic_slice(weight, (0, start), (weight.shape[0], count))

    def both(start, count):
        return jnp.concatenate(
            [columns(gate_weight, start, count), columns(up_weight, start, count)], axis=1
        )

    other = (1 - x_lo) * half
    own = x_lo * half
    away_a = both(other, part_a)
    away_b = both(other + part_a, part_b)

    one_hot = (
        lang_ids[:, None] == jnp.arange(gain_table.shape[0], dtype=jnp.int32)[None, :]
    ).astype(F32)
    token_gains = jnp.dot(one_hot, gain_table, precision=lax.Precision.HIGHEST)
    values = tokens.astype(F32)
    scaled = (values * token_gains).astype(BF)
    squares = jnp.sum(values * values, axis=1, keepdims=True)
    high, low = high_low(squares)
    pad = jnp.zeros((rows, 126), BF)
    block = jnp.concatenate([scaled, high, low, pad], axis=1)
    block = lax.dynamic_slice(
        jnp.concatenate([block, block], axis=0), (z * 8, 0), block.shape
    ).reshape(8, 8, width + 128)

    from_1, from_2, from_3 = (swap_x(block, bits) for bits in (1, 2, 3))
    block = jnp.concatenate(
        [
            jnp.concatenate([block, from_2], axis=1),
            jnp.concatenate([from_1, from_3], axis=1),
        ],
        axis=2,
    )
    block, away_a = tie(block, away_a)
    from_1, from_2, from_3 = (swap_y(block, bits) for bits in (1, 2, 3))
    piece_a = swap_x(away_a, 1)
    from_1, from_2, from_3, piece_a, away_b = tie(from_1, from_2, from_3, piece_a, away_b)
    block = jnp.concatenate([block, from_1, from_2, from_3], axis=1)
    piece_b = swap_x(away_b[:288], 1)
    from_core = swap_core(block)
    from_core, piece_b, rest_b = tie(from_core, piece_b, away_b[288:])
    piece_c = swap_x(rest_b, 1)
    block = jnp.concatenate([block, from_core], axis=1)
    edge = width + 128
    here = block[:, :, :width].reshape(-1, width)
    there = block[:, :, edge : edge + width].reshape(-1, width)
    everything = jnp.concatenate([here, there], axis=1)
    square_sums = add(
        block[:, :, width],
        block[:, :, width + 1],
        block[:, :, edge + width],
        block[:, :, edge + width + 1],
    )

    weight_a = jnp.concatenate([both(own, part_a), piece_a], axis=0)
    sums_a = (
        jnp.dot(everything, weight_a, preferred_element_type=F32)
        .astype(BF)
        .reshape(8, -1, 2 * part_a)
    )
    weight_b = jnp.concatenate([both(own + part_a, part_b), piece_b, piece_c], axis=0)
    sums_b = (
        jnp.dot(everything, weight_b, preferred_element_type=F32)
        .astype(BF)
        .reshape(8, -1, 2 * part_b)
    )

    cut = 2 * part_a

    def with_squares(k, arrived=None):
        total = square_sums[k][:, None]
        if arrived is None:
            body = sums_a[k]
        else:
            body = add(sums_a[k], arrived[:, :cut]).astype(BF)
            total = total + add(arrived[:, cut : cut + 1], arrived[:, cut + 1 : cut + 2])
        high, low = high_low(total)
        return jnp.concatenate([body, high, low, jnp.zeros((body.shape[0], 126), BF)], axis=1)

    def pair(send_up, send_down):
        send_up, send_down = tie(send_up, send_down)
        return tie(shift_z(send_up, 1), shift_z(send_down, -1))

    up_a = shift_z(with_squares(4), 1)
    down_b = shift_z(sums_b[4], -1)
    down_a = up_b = None
    for hop in (1, 2, 3):
        up_a, down_a = pair(with_squares(4 - hop, up_a), with_squares(4 + hop, down_a))
        if hop == 1:
            up_a, down_a, down_b = tie(up_a, down_a, down_b)
        if hop == 2:
            up_a, down_weight = tie(up_a, down_weight)
        send_up = sums_b[3] if up_b is None else add(sums_b[4 - hop], up_b).astype(BF)
        up_b, down_b = pair(send_up, add(sums_b[4 + hop], down_b).astype(BF))

    all_squares = square_sums[0][:, None] + add(
        up_a[:, cut : cut + 1],
        up_a[:, cut + 1 : cut + 2],
        down_a[:, cut : cut + 1],
        down_a[:, cut + 1 : cut + 2],
    )
    inverse_rms = lax.rsqrt(all_squares / (width * 16) + 1e-05)

    def activate(summed, count):
        gate = summed[:, :count] * inverse_rms
        up = summed[:, count:] * inverse_rms
        return (jax.nn.silu(gate) * up).astype(BF)

    hidden_a = activate(add(sums_a[0], up_a[:, :cut], down_a[:, :cut]), part_a)
    hidden_b = activate(add(sums_b[0], up_b, down_b), part_b)

    down_there = swap_x(lax.dynamic_slice(down_weight, (other, 0), (half, width)), 1)
    down_here = lax.dynamic_slice(down_weight, (own, 0), (half, width))
    down_both = jnp.concatenate([down_here, down_there], axis=1)

    def project(hidden):
        terms = jnp.dot(
            jnp.concatenate([jnp.concatenate(chunk, axis=1) for chunk in hidden], axis=0),
            down_both,
            preferred_element_type=F32,
        )
        return terms.astype(BF).reshape(len(hidden), 128, 2 * width)

    def sum_core(terms):
        return add(terms[:, :64], swap_core(terms[:, 64:])).astype(BF)

    def sum_y(terms):
        return add(
            terms[:, :16],
            swap_y(terms[:, 16:32], 1),
            swap_y(terms[:, 32:48], 2),
            swap_y(terms[:, 48:64], 3),
        ).astype(BF)

    def sum_x(terms):
        return add(
            terms[:, :8, :width],
            swap_x(terms[:, :8, width:], 1),
            swap_x(terms[:, 8:, :width], 2),
            swap_x(terms[:, 8:, width:], 3),
        )

    chunks = {0: (hidden_a, hidden_b)}
    up, down = chunks[0], chunks[0]
    for step in (1, 2, 3):
        up_a, down_a = pair(up[0], down[0])
        up_b, down_b = pair(up[1], down[1])
        up, down = (up_a, up_b), (down_a, down_b)
        chunks[8 - step] = up
        chunks[step] = down
    first = project([chunks[k] for k in (6, 7, 0, 1, 2)])
    first, last_up, last_down = tie(first, up[0], down[1])
    first = sum_core(first)
    chunks[4] = tie(shift_z(last_up, 1), shift_z(last_down, -1))
    first, last_a, last_b = tie(first, *chunks[4])
    first = sum_y(first)
    second = project([chunks[3], (last_a, last_b), chunks[5]])
    second = sum_y(sum_core(second))
    own_rows = jnp.concatenate([sum_x(first), sum_x(second)], axis=0).reshape(rows, width)
    own_rows = lax.dynamic_slice(
        jnp.concatenate([own_rows, own_rows], axis=0), ((10 - z) % 8 * 8, 0), (rows, width)
    )
    return (values + own_rows).astype(BF)


def solution(mesh):
    return jax.shard_map(
        local,
        mesh=mesh,
        in_specs=(
            P("ffn", "hid"),
            P("ffn"),
            P(None, "hid"),
            P("hid", "ffn"),
            P("hid", "ffn"),
            P("ffn", "hid"),
        ),
        out_specs=P("ffn", "hid"),
        check_vma=False,
    )
```

```python
import jax
import jax.numpy as jnp
from jax import lax
from jax.sharding import PartitionSpec as P

AXES = ("hid", "ffn")
BF = jnp.bfloat16
F32 = jnp.float32


def permutation(move):
    pairs = []
    for xl in range(2):
        for z in range(8):
            for xh in range(2):
                for y in range(4):
                    for core in range(2):
                        x, yy, zz, cc = move(xh * 2 + xl, y, z, core)
                        source = (xl * 8 + z) * 16 + xh * 8 + y * 2 + core
                        target = ((x % 2) * 8 + zz) * 16 + (x // 2) * 8 + yy * 2 + cc
                        pairs.append((source, target))
    return pairs


def swap_x(value, bits):
    return lax.ppermute(value, AXES, permutation(lambda x, y, z, c: (x ^ bits, y, z, c)))


def swap_y(value, bits):
    return lax.ppermute(value, AXES, permutation(lambda x, y, z, c: (x, y ^ bits, z, c)))


def swap_core(value):
    return lax.ppermute(value, AXES, permutation(lambda x, y, z, c: (x, y, z, c ^ 1)))


def shift_z(value, step):
    return lax.ppermute(value, AXES, permutation(lambda x, y, z, c: (x, y, (z + step) % 8, c)))


def tie(*values):
    return lax.optimization_barrier(values)


def add(*terms):
    total = terms[0].astype(F32)
    for term in terms[1:]:
        total = total + term.astype(F32)
    return total


def high_low(value):
    high = value.astype(BF)
    low = (value - high.astype(F32)).astype(BF)
    return high, low


def local(tokens, lang_ids, gain_table, gate_weight, up_weight, down_weight):
    rows, width = tokens.shape
    units = gate_weight.shape[1]
    half = units // 2
    part_a = half - 512
    part_b = half - part_a
    hid = lax.axis_index("hid")
    x_lo, z = hid // 8, hid % 8

    def pick(weight, start, count, mine):
        low = weight[:, start : start + count]
        high = weight[:, half + start : half + start + count]
        return jnp.where((x_lo == 0) == mine, low, high)

    def both(start, count, mine):
        return jnp.concatenate(
            [pick(gate_weight, start, count, mine), pick(up_weight, start, count, mine)], axis=1
        )

    away_a = both(0, part_a, False)
    away_b = both(part_a, part_b, False)

    one_hot = (
        lang_ids[:, None] == jnp.arange(gain_table.shape[0], dtype=jnp.int32)[None, :]
    ).astype(F32)
    token_gains = jnp.dot(one_hot, gain_table, precision=lax.Precision.HIGHEST)
    values = tokens.astype(F32)
    scaled = (values * token_gains).astype(BF)
    squares = jnp.sum(values * values, axis=1, keepdims=True)
    high, low = high_low(squares)
    pad = jnp.zeros((rows, 126), BF)
    block = jnp.concatenate([scaled, high, low, pad], axis=1)
    block = lax.dynamic_slice(
        jnp.concatenate([block, block], axis=0), (z * 8, 0), block.shape
    ).reshape(8, 8, width + 128)

    from_1, from_2, from_3 = (swap_x(block, bits) for bits in (1, 2, 3))
    piece_a0 = swap_x(away_a[:64], 1)
    from_1, from_2, from_3, piece_a0, away_a, away_b = tie(
        from_1, from_2, from_3, piece_a0, away_a, away_b
    )
    block = jnp.concatenate(
        [
            jnp.concatenate([block, from_2], axis=1),
            jnp.concatenate([from_1, from_3], axis=1),
        ],
        axis=2,
    )
    from_1, from_2, from_3 = (swap_y(block, bits) for bits in (1, 2, 3))
    piece_a1 = swap_x(away_a[64:], 1)
    piece_b0 = swap_x(away_b[:192], 1)
    from_1, from_2, from_3, piece_a1, piece_b0, away_b = tie(
        from_1, from_2, from_3, piece_a1, piece_b0, away_b
    )
    block = jnp.concatenate([block, from_1, from_2, from_3], axis=1)
    piece_b1 = swap_x(away_b[192:384], 1)
    from_core = swap_core(block)
    from_core, piece_b1, rest_b = tie(from_core, piece_b1, away_b[384:])
    piece_b2 = swap_x(rest_b, 1)
    block = jnp.concatenate([block, from_core], axis=1)
    edge = width + 128
    here = block[:, :, :width].reshape(-1, width)
    there = block[:, :, edge : edge + width].reshape(-1, width)
    everything = jnp.concatenate([here, there], axis=1)
    square_sums = add(
        block[:, :, width],
        block[:, :, width + 1],
        block[:, :, edge + width],
        block[:, :, edge + width + 1],
    )

    weight_a = jnp.concatenate([both(0, part_a, True), piece_a0, piece_a1], axis=0)
    sums_a = (
        jnp.dot(everything, weight_a, preferred_element_type=F32)
        .astype(BF)
        .reshape(8, -1, 2 * part_a)
    )
    weight_b = jnp.concatenate([both(part_a, part_b, True), piece_b0, piece_b1, piece_b2], axis=0)
    sums_b = (
        jnp.dot(everything, weight_b, preferred_element_type=F32)
        .astype(BF)
        .reshape(8, -1, 2 * part_b)
    )

    cut = 2 * part_a

    def with_squares(k, arrived=None):
        total = square_sums[k][:, None]
        if arrived is None:
            body = sums_a[k]
        else:
            body = add(sums_a[k], arrived[:, :cut]).astype(BF)
            total = total + add(arrived[:, cut : cut + 1], arrived[:, cut + 1 : cut + 2])
        high, low = high_low(total)
        return jnp.concatenate([body, high, low, jnp.zeros((body.shape[0], 126), BF)], axis=1)

    def pair(send_up, send_down):
        send_up, send_down = tie(send_up, send_down)
        return tie(shift_z(send_up, 1), shift_z(send_down, -1))

    up_a = shift_z(with_squares(4), 1)
    down_b = shift_z(sums_b[4], -1)
    down_a = up_b = None
    for hop in (1, 2, 3):
        up_a, down_a = pair(with_squares(4 - hop, up_a), with_squares(4 + hop, down_a))
        if hop == 1:
            up_a, down_a, down_b = tie(up_a, down_a, down_b)
        if hop == 2:
            up_a, down_weight = tie(up_a, down_weight)
        send_up = sums_b[3] if up_b is None else add(sums_b[4 - hop], up_b).astype(BF)
        up_b, down_b = pair(send_up, add(sums_b[4 + hop], down_b).astype(BF))

    all_squares = square_sums[0][:, None] + add(
        up_a[:, cut : cut + 1],
        up_a[:, cut + 1 : cut + 2],
        down_a[:, cut : cut + 1],
        down_a[:, cut + 1 : cut + 2],
    )
    inverse_rms = lax.rsqrt(all_squares / (width * 16) + 1e-05)

    def activate(summed, count):
        gate = summed[:, :count] * inverse_rms
        up = summed[:, count:] * inverse_rms
        return (jax.nn.silu(gate) * up).astype(BF)

    hidden_a = activate(add(sums_a[0], up_a[:, :cut], down_a[:, :cut]), part_a)
    hidden_b = activate(add(sums_b[0], up_b, down_b), part_b)

    down_low, down_high = down_weight[:half], down_weight[half:]
    down_there = swap_x(jnp.where(x_lo == 0, down_high, down_low), 1)
    down_here = jnp.where(x_lo == 0, down_low, down_high)
    down_both = jnp.concatenate([down_here, down_there], axis=1)

    def project(hidden):
        terms = jnp.dot(
            jnp.concatenate([jnp.concatenate(chunk, axis=1) for chunk in hidden], axis=0),
            down_both,
            preferred_element_type=F32,
        )
        return terms.astype(BF).reshape(len(hidden), 128, 2 * width)

    def sum_core(terms):
        return add(terms[:, :64], swap_core(terms[:, 64:])).astype(BF)

    def sum_y(terms):
        return add(
            terms[:, :16],
            swap_y(terms[:, 16:32], 1),
            swap_y(terms[:, 32:48], 2),
            swap_y(terms[:, 48:64], 3),
        ).astype(BF)

    def sum_x(terms):
        return add(
            terms[:, :8, :width],
            swap_x(terms[:, :8, width:], 1),
            swap_x(terms[:, 8:, :width], 2),
            swap_x(terms[:, 8:, width:], 3),
        )

    chunks = {0: (hidden_a, hidden_b)}
    near = []
    for part in chunks[0]:
        near.append(tie(*(shift_z(part, step) for step in (1, -1, 2, -2))))
    for place, k in enumerate((7, 1, 6, 2)):
        chunks[k] = (near[0][place], near[1][place])
    below_a, below_b, above_a, above_b = tie(*chunks[6], *chunks[2])
    far = [
        shift_z(below_a, 1),
        shift_z(above_a, -1),
        shift_z(above_a, -2),
        shift_z(below_b, 1),
        shift_z(above_b, -1),
        shift_z(below_b, 2),
    ]
    first = sum_core(project([chunks[k] for k in (6, 7, 0, 1, 2)]))
    first, *far = tie(first, *far)
    chunks[5], chunks[3], chunks[4] = (far[0], far[3]), (far[1], far[4]), (far[2], far[5])
    first = sum_y(first)
    second = project([chunks[3], chunks[4], chunks[5]])
    second = sum_y(sum_core(second))
    own_rows = jnp.concatenate([sum_x(first), sum_x(second)], axis=0).reshape(rows, width)
    own_rows = lax.dynamic_slice(
        jnp.concatenate([own_rows, own_rows], axis=0), ((10 - z) % 8 * 8, 0), (rows, width)
    )
    return (values + own_rows).astype(BF)


def solution(mesh):
    return jax.shard_map(
        local,
        mesh=mesh,
        in_specs=(
            P("ffn", "hid"),
            P("ffn"),
            P(None, "hid"),
            P("hid", "ffn"),
            P("hid", "ffn"),
            P("ffn", "hid"),
        ),
        out_specs=P("ffn", "hid"),
        check_vma=False,
    )
```

```python
import jax
import jax.numpy as jnp
from jax import lax
from jax.sharding import PartitionSpec as P

AXES = ("hid", "ffn")
BF = jnp.bfloat16
F32 = jnp.float32


def permutation(move):
    pairs = []
    for xl in range(2):
        for z in range(8):
            for xh in range(2):
                for y in range(4):
                    for core in range(2):
                        x, yy, zz, cc = move(xh * 2 + xl, y, z, core)
                        source = (xl * 8 + z) * 16 + xh * 8 + y * 2 + core
                        target = ((x % 2) * 8 + zz) * 16 + (x // 2) * 8 + yy * 2 + cc
                        pairs.append((source, target))
    return pairs


def swap_x(value, bits):
    return lax.ppermute(value, AXES, permutation(lambda x, y, z, c: (x ^ bits, y, z, c)))


def swap_y(value, bits):
    return lax.ppermute(value, AXES, permutation(lambda x, y, z, c: (x, y ^ bits, z, c)))


def swap_core(value):
    return lax.ppermute(value, AXES, permutation(lambda x, y, z, c: (x, y, z, c ^ 1)))


def shift_z(value, step):
    return lax.ppermute(value, AXES, permutation(lambda x, y, z, c: (x, y, (z + step) % 8, c)))


def tie(*values):
    return lax.optimization_barrier(values)


def add(*terms):
    total = terms[0].astype(F32)
    for term in terms[1:]:
        total = total + term.astype(F32)
    return total


def high_low(value):
    high = value.astype(BF)
    low = (value - high.astype(F32)).astype(BF)
    return high, low


def local(tokens, lang_ids, gain_table, gate_weight, up_weight, down_weight):
    rows, width = tokens.shape
    units = gate_weight.shape[1]
    half = units // 2
    part_a = half - 512
    part_b = half - part_a
    hid = lax.axis_index("hid")
    x_lo, z = hid // 8, hid % 8

    def pick(weight, start, count, mine):
        low = weight[:, start : start + count]
        high = weight[:, half + start : half + start + count]
        return jnp.where((x_lo == 0) == mine, low, high)

    def both(start, count, mine):
        return jnp.concatenate(
            [pick(gate_weight, start, count, mine), pick(up_weight, start, count, mine)], axis=1
        )

    away_a = both(0, part_a, False)
    away_b = both(part_a, part_b, False)

    one_hot = (
        lang_ids[:, None] == jnp.arange(gain_table.shape[0], dtype=jnp.int32)[None, :]
    ).astype(F32)
    token_gains = jnp.dot(one_hot, gain_table, precision=lax.Precision.HIGHEST)
    values = tokens.astype(F32)
    scaled = (values * token_gains).astype(BF)
    squares = jnp.sum(values * values, axis=1, keepdims=True)
    high, low = high_low(squares)
    pad = jnp.zeros((rows, 126), BF)
    block = jnp.concatenate([scaled, high, low, pad], axis=1)
    block = lax.dynamic_slice(
        jnp.concatenate([block, block], axis=0), (z * 8, 0), block.shape
    ).reshape(8, 8, width + 128)

    from_1, from_2, from_3 = (swap_x(block, bits) for bits in (1, 2, 3))
    piece_a0 = swap_x(away_a[:64], 1)
    from_1, from_2, from_3, piece_a0, away_a, away_b = tie(
        from_1, from_2, from_3, piece_a0, away_a, away_b
    )
    block = jnp.concatenate(
        [
            jnp.concatenate([block, from_2], axis=1),
            jnp.concatenate([from_1, from_3], axis=1),
        ],
        axis=2,
    )
    from_1, from_2, from_3 = (swap_y(block, bits) for bits in (1, 2, 3))
    piece_a1 = swap_x(away_a[64:], 1)
    piece_b0 = swap_x(away_b[:192], 1)
    from_1, from_2, from_3, piece_a1, piece_b0, away_b = tie(
        from_1, from_2, from_3, piece_a1, piece_b0, away_b
    )
    block = jnp.concatenate([block, from_1, from_2, from_3], axis=1)
    from_core = swap_core(block)
    piece_b1 = swap_x(away_b[192:], 1)
    block = jnp.concatenate([block, from_core], axis=1)
    edge = width + 128
    here = block[:, :, :width].reshape(-1, width)
    there = block[:, :, edge : edge + width].reshape(-1, width)
    everything = jnp.concatenate([here, there], axis=1)
    square_sums = add(
        block[:, :, width],
        block[:, :, width + 1],
        block[:, :, edge + width],
        block[:, :, edge + width + 1],
    )

    weight_a = jnp.concatenate([both(0, part_a, True), piece_a0, piece_a1], axis=0)
    sums_a = (
        jnp.dot(everything, weight_a, preferred_element_type=F32)
        .astype(BF)
        .reshape(8, -1, 2 * part_a)
    )
    weight_b = jnp.concatenate([both(part_a, part_b, True), piece_b0, piece_b1], axis=0)
    sums_b = (
        jnp.dot(everything, weight_b, preferred_element_type=F32)
        .astype(BF)
        .reshape(8, -1, 2 * part_b)
    )

    cut = 2 * part_a

    def with_squares(k, arrived=None):
        total = square_sums[k][:, None]
        if arrived is None:
            body = sums_a[k]
        else:
            body = add(sums_a[k], arrived[:, :cut]).astype(BF)
            total = total + add(arrived[:, cut : cut + 1], arrived[:, cut + 1 : cut + 2])
        high, low = high_low(total)
        return jnp.concatenate([body, high, low, jnp.zeros((body.shape[0], 126), BF)], axis=1)

    def pair(send_up, send_down):
        send_up, send_down = tie(send_up, send_down)
        return tie(shift_z(send_up, 1), shift_z(send_down, -1))

    up_a = shift_z(with_squares(4), 1)
    down_b = shift_z(sums_b[4], -1)
    down_a = up_b = None
    for hop in (1, 2, 3):
        up_a, down_a = pair(with_squares(4 - hop, up_a), with_squares(4 + hop, down_a))
        if hop == 1:
            up_a, down_a, down_b = tie(up_a, down_a, down_b)
        if hop == 2:
            up_a, down_weight = tie(up_a, down_weight)
        send_up = sums_b[3] if up_b is None else add(sums_b[4 - hop], up_b).astype(BF)
        up_b, down_b = pair(send_up, add(sums_b[4 + hop], down_b).astype(BF))

    all_squares = square_sums[0][:, None] + add(
        up_a[:, cut : cut + 1],
        up_a[:, cut + 1 : cut + 2],
        down_a[:, cut : cut + 1],
        down_a[:, cut + 1 : cut + 2],
    )
    inverse_rms = lax.rsqrt(all_squares / (width * 16) + 1e-05)

    def activate(summed, count):
        gate = summed[:, :count] * inverse_rms
        up = summed[:, count:] * inverse_rms
        return (jax.nn.silu(gate) * up).astype(BF)

    hidden_a = activate(add(sums_a[0], up_a[:, :cut], down_a[:, :cut]), part_a)
    up_1, down_1, up_b, down_b = tie(
        shift_z(hidden_a, 1), shift_z(hidden_a, -1), up_b, down_b
    )
    hidden_b = activate(add(sums_b[0], up_b, down_b), part_b)

    down_low, down_high = down_weight[:half], down_weight[half:]
    down_there = swap_x(jnp.where(x_lo == 0, down_high, down_low), 1)
    down_here = jnp.where(x_lo == 0, down_low, down_high)
    down_both = jnp.concatenate([down_here, down_there], axis=1)

    def project(hidden):
        terms = jnp.dot(
            jnp.concatenate([jnp.concatenate(chunk, axis=1) for chunk in hidden], axis=0),
            down_both,
            preferred_element_type=F32,
        )
        return terms.astype(BF).reshape(len(hidden), 128, 2 * width)

    def sum_core(terms):
        return add(terms[:, :64], swap_core(terms[:, 64:])).astype(BF)

    def sum_y(terms):
        return add(
            terms[:, :16],
            swap_y(terms[:, 16:32], 1),
            swap_y(terms[:, 32:48], 2),
            swap_y(terms[:, 48:64], 3),
        ).astype(BF)

    def sum_x(terms):
        return add(
            terms[:, :8, :width],
            swap_x(terms[:, :8, width:], 1),
            swap_x(terms[:, 8:, :width], 2),
            swap_x(terms[:, 8:, width:], 3),
        )

    chunks = {0: (hidden_a, hidden_b)}
    up = (up_1, shift_z(hidden_b, 1))
    down = (down_1, shift_z(hidden_b, -1))
    chunks[7], chunks[1] = up, down
    for step in (2, 3):
        up = (shift_z(up[0], 1), shift_z(up[1], 1))
        down = (shift_z(down[0], -1), shift_z(down[1], -1))
        chunks[8 - step] = up
        chunks[step] = down
    chunks[4] = (shift_z(up[0], 1), shift_z(down[1], -1))
    first = sum_core(project([chunks[k] for k in (6, 7, 0, 1, 2)]))
    first, chunks[4] = tie(first, chunks[4])
    first = sum_y(first)
    second = project([chunks[3], chunks[4], chunks[5]])
    second = sum_y(sum_core(second))
    own_rows = jnp.concatenate([sum_x(first), sum_x(second)], axis=0).reshape(rows, width)
    own_rows = lax.dynamic_slice(
        jnp.concatenate([own_rows, own_rows], axis=0), ((10 - z) % 8 * 8, 0), (rows, width)
    )
    return (values + own_rows).astype(BF)


def solution(mesh):
    return jax.shard_map(
        local,
        mesh=mesh,
        in_specs=(
            P("ffn", "hid"),
            P("ffn"),
            P(None, "hid"),
            P("hid", "ffn"),
            P("hid", "ffn"),
            P("ffn", "hid"),
        ),
        out_specs=P("ffn", "hid"),
        check_vma=False,
    )
```

```python
import jax
import jax.numpy as jnp
from jax import lax
from jax.sharding import PartitionSpec as P

AXES = ("hid", "ffn")
BF = jnp.bfloat16
F32 = jnp.float32


def permutation(move):
    pairs = []
    for xl in range(2):
        for z in range(8):
            for xh in range(2):
                for y in range(4):
                    for core in range(2):
                        x, yy, zz, cc = move(xh * 2 + xl, y, z, core)
                        source = (xl * 8 + z) * 16 + xh * 8 + y * 2 + core
                        target = ((x % 2) * 8 + zz) * 16 + (x // 2) * 8 + yy * 2 + cc
                        pairs.append((source, target))
    return pairs


def swap_x(value, bits):
    return lax.ppermute(value, AXES, permutation(lambda x, y, z, c: (x ^ bits, y, z, c)))


def swap_y(value, bits):
    return lax.ppermute(value, AXES, permutation(lambda x, y, z, c: (x, y ^ bits, z, c)))


def swap_core(value):
    return lax.ppermute(value, AXES, permutation(lambda x, y, z, c: (x, y, z, c ^ 1)))


def shift_z(value, step):
    return lax.ppermute(value, AXES, permutation(lambda x, y, z, c: (x, y, (z + step) % 8, c)))


def tie(*values):
    return lax.optimization_barrier(values)


def add(*terms):
    total = terms[0].astype(F32)
    for term in terms[1:]:
        total = total + term.astype(F32)
    return total


def high_low(value):
    high = value.astype(BF)
    low = (value - high.astype(F32)).astype(BF)
    return high, low


def local(tokens, lang_ids, gain_table, gate_weight, up_weight, down_weight):
    rows, width = tokens.shape
    units = gate_weight.shape[1]
    half = units // 2
    part_a = half - 512
    part_b = half - part_a
    hid = lax.axis_index("hid")
    x_lo, z = hid // 8, hid % 8

    def pick(weight, start, count, mine):
        low = weight[:, start : start + count]
        high = weight[:, half + start : half + start + count]
        return jnp.where((x_lo == 0) == mine, low, high)

    def both(start, count, mine, first=0, last=None):
        return jnp.concatenate(
            [
                pick(gate_weight[first:last], start, count, mine),
                pick(up_weight[first:last], start, count, mine),
            ],
            axis=1,
        )

    away_a0 = both(0, part_a, False, 0, 224)
    away_a1 = both(0, part_a, False, 224)
    away_b0 = both(part_a, part_b, False, 0, 320)
    away_b1 = both(part_a, part_b, False, 320)

    one_hot = (
        lang_ids[:, None] == jnp.arange(gain_table.shape[0], dtype=jnp.int32)[None, :]
    ).astype(F32)
    token_gains = jnp.dot(one_hot, gain_table, precision=lax.Precision.HIGHEST)
    values = tokens.astype(F32)
    scaled = (values * token_gains).astype(BF)
    squares = jnp.sum(values * values, axis=1, keepdims=True)
    high, low = high_low(squares)
    pad = jnp.zeros((rows, 126), BF)
    block = jnp.concatenate([scaled, high, low, pad], axis=1)
    block = lax.dynamic_slice(
        jnp.concatenate([block, block], axis=0), (z * 8, 0), block.shape
    ).reshape(8, 8, width + 128)

    from_1, from_2, from_3 = (swap_x(block, bits) for bits in (1, 2, 3))
    piece_a0 = swap_x(away_a0, 1)
    from_1, from_2, from_3, piece_a0, away_a1, away_b0 = tie(
        from_1, from_2, from_3, piece_a0, away_a1, away_b0
    )
    block = jnp.concatenate(
        [
            jnp.concatenate([block, from_2], axis=1),
            jnp.concatenate([from_1, from_3], axis=1),
        ],
        axis=2,
    )
    from_1, from_2, from_3 = (swap_y(block, bits) for bits in (1, 2, 3))
    piece_a1 = swap_x(away_a1, 1)
    piece_b0 = swap_x(away_b0, 1)
    from_1, from_2, from_3, piece_a1, piece_b0, away_b1 = tie(
        from_1, from_2, from_3, piece_a1, piece_b0, away_b1
    )
    block = jnp.concatenate([block, from_1, from_2, from_3], axis=1)
    from_core = swap_core(block)
    piece_b1 = swap_x(away_b1, 1)
    block = jnp.concatenate([block, from_core], axis=1)
    edge = width + 128
    here = block[:, :, :width].reshape(-1, width)
    there = block[:, :, edge : edge + width].reshape(-1, width)
    everything = jnp.concatenate([here, there], axis=1)
    square_sums = add(
        block[:, :, width],
        block[:, :, width + 1],
        block[:, :, edge + width],
        block[:, :, edge + width + 1],
    )

    weight_a = jnp.concatenate([both(0, part_a, True), piece_a0, piece_a1], axis=0)
    sums_a = (
        jnp.dot(everything, weight_a, preferred_element_type=F32)
        .astype(BF)
        .reshape(8, -1, 2 * part_a)
    )
    weight_b = jnp.concatenate([both(part_a, part_b, True), piece_b0, piece_b1], axis=0)
    sums_b = (
        jnp.dot(everything, weight_b, preferred_element_type=F32)
        .astype(BF)
        .reshape(8, -1, 2 * part_b)
    )

    cut = 2 * part_a

    def with_squares(k, arrived=None):
        total = square_sums[k][:, None]
        if arrived is None:
            body = sums_a[k]
        else:
            body = add(sums_a[k], arrived[:, :cut]).astype(BF)
            total = total + add(arrived[:, cut : cut + 1], arrived[:, cut + 1 : cut + 2])
        high, low = high_low(total)
        return jnp.concatenate([body, high, low, jnp.zeros((body.shape[0], 126), BF)], axis=1)

    def pair(send_up, send_down):
        send_up, send_down = tie(send_up, send_down)
        return tie(shift_z(send_up, 1), shift_z(send_down, -1))

    up_a = shift_z(with_squares(4), 1)
    down_b = shift_z(sums_b[4], -1)
    down_a = up_b = None
    for hop in (1, 2, 3):
        up_a, down_a = pair(with_squares(4 - hop, up_a), with_squares(4 + hop, down_a))
        if hop == 1:
            up_a, down_a, down_b = tie(up_a, down_a, down_b)
        if hop == 2:
            up_a, down_weight = tie(up_a, down_weight)
        send_up = sums_b[3] if up_b is None else add(sums_b[4 - hop], up_b).astype(BF)
        up_b, down_b = pair(send_up, add(sums_b[4 + hop], down_b).astype(BF))

    all_squares = square_sums[0][:, None] + add(
        up_a[:, cut : cut + 1],
        up_a[:, cut + 1 : cut + 2],
        down_a[:, cut : cut + 1],
        down_a[:, cut + 1 : cut + 2],
    )
    inverse_rms = lax.rsqrt(all_squares / (width * 16) + 1e-05)

    def activate(summed, count):
        gate = summed[:, :count] * inverse_rms
        up = summed[:, count:] * inverse_rms
        return (jax.nn.silu(gate) * up).astype(BF)

    hidden_a = activate(add(sums_a[0], up_a[:, :cut], down_a[:, :cut]), part_a)
    up_1, down_1, up_b, down_b = tie(
        shift_z(hidden_a, 1), shift_z(hidden_a, -1), up_b, down_b
    )
    hidden_b = activate(add(sums_b[0], up_b, down_b), part_b)

    down_low, down_high = down_weight[:half], down_weight[half:]
    down_there = swap_x(jnp.where(x_lo == 0, down_high, down_low), 1)
    down_here = jnp.where(x_lo == 0, down_low, down_high)
    down_both = jnp.concatenate([down_here, down_there], axis=1)

    def project(hidden):
        terms = jnp.dot(
            jnp.concatenate([jnp.concatenate(chunk, axis=1) for chunk in hidden], axis=0),
            down_both,
            preferred_element_type=F32,
        )
        return terms.astype(BF).reshape(len(hidden), 128, 2 * width)

    def sum_core(terms):
        return add(terms[:, :64], swap_core(terms[:, 64:])).astype(BF)

    def sum_y(terms):
        return add(
            terms[:, :16],
            swap_y(terms[:, 16:32], 1),
            swap_y(terms[:, 32:48], 2),
            swap_y(terms[:, 48:64], 3),
        ).astype(BF)

    def sum_x(terms):
        return add(
            terms[:, :8, :width],
            swap_x(terms[:, :8, width:], 1),
            swap_x(terms[:, 8:, :width], 2),
            swap_x(terms[:, 8:, width:], 3),
        )

    chunks = {0: (hidden_a, hidden_b)}
    up = (up_1, shift_z(hidden_b, 1))
    down = (down_1, shift_z(hidden_b, -1))
    chunks[7], chunks[1] = up, down
    for step in (2, 3):
        up = (shift_z(up[0], 1), shift_z(up[1], 1))
        down = (shift_z(down[0], -1), shift_z(down[1], -1))
        chunks[8 - step] = up
        chunks[step] = down
    chunks[4] = (shift_z(up[0], 1), shift_z(down[1], -1))
    first = sum_core(project([chunks[k] for k in (6, 7, 0, 1, 2)]))
    first, chunks[4] = tie(first, chunks[4])
    first = sum_y(first)
    second = project([chunks[3], chunks[4], chunks[5]])
    second = sum_core(second).reshape(3, 4, 2, 8, 2 * width)
    second = add(
        second[:, :, 0, :, :width],
        swap_x(second[:, :, 0, :, width:], 1),
        swap_x(second[:, :, 1, :, :width], 2),
        swap_x(second[:, :, 1, :, width:], 3),
    ).astype(BF)
    second = add(second[:, 0], *(swap_y(second[:, bits], bits) for bits in (1, 2, 3)))
    own_rows = jnp.concatenate([sum_x(first), second], axis=0).reshape(rows, width)
    own_rows = lax.dynamic_slice(
        jnp.concatenate([own_rows, own_rows], axis=0), ((10 - z) % 8 * 8, 0), (rows, width)
    )
    return (values + own_rows).astype(BF)


def solution(mesh):
    return jax.shard_map(
        local,
        mesh=mesh,
        in_specs=(
            P("ffn", "hid"),
            P("ffn"),
            P(None, "hid"),
            P("hid", "ffn"),
            P("hid", "ffn"),
            P("ffn", "hid"),
        ),
        out_specs=P("ffn", "hid"),
        check_vma=False,
    )
```

```python
import jax
import jax.numpy as jnp
from jax import lax
from jax.sharding import PartitionSpec as P

AXES = ("hid", "ffn")
BF = jnp.bfloat16
F32 = jnp.float32


def permutation(move):
    pairs = []
    for xl in range(2):
        for z in range(8):
            for xh in range(2):
                for y in range(4):
                    for core in range(2):
                        x, yy, zz, cc = move(xh * 2 + xl, y, z, core)
                        source = (xl * 8 + z) * 16 + xh * 8 + y * 2 + core
                        target = ((x % 2) * 8 + zz) * 16 + (x // 2) * 8 + yy * 2 + cc
                        pairs.append((source, target))
    return pairs


def swap_x(value, bits):
    return lax.ppermute(value, AXES, permutation(lambda x, y, z, c: (x ^ bits, y, z, c)))


def swap_y(value, bits):
    return lax.ppermute(value, AXES, permutation(lambda x, y, z, c: (x, y ^ bits, z, c)))


def swap_core(value):
    return lax.ppermute(value, AXES, permutation(lambda x, y, z, c: (x, y, z, c ^ 1)))


def shift_z(value, step):
    return lax.ppermute(value, AXES, permutation(lambda x, y, z, c: (x, y, (z + step) % 8, c)))


def tie(*values):
    return lax.optimization_barrier(values)


def add(*terms):
    total = terms[0].astype(F32)
    for term in terms[1:]:
        total = total + term.astype(F32)
    return total


def high_low(value):
    high = value.astype(BF)
    low = (value - high.astype(F32)).astype(BF)
    return high, low


def local(tokens, lang_ids, gain_table, gate_weight, up_weight, down_weight):
    rows, width = tokens.shape
    units = gate_weight.shape[1]
    half = units // 2
    part_a = half - 256
    part_b = half - part_a
    hid = lax.axis_index("hid")
    x_lo, z = hid // 8, hid % 8

    def pick(weight, start, count, mine):
        low = weight[:, start : start + count]
        high = weight[:, half + start : half + start + count]
        return jnp.where((x_lo == 0) == mine, low, high)

    def both(start, count, mine, first=0, last=None):
        return jnp.concatenate(
            [
                pick(gate_weight[first:last], start, count, mine),
                pick(up_weight[first:last], start, count, mine),
            ],
            axis=1,
        )

    away_a0 = both(0, part_a, False, 0, 96)
    away_a1 = both(0, part_a, False, 96)
    away_b = both(part_a, part_b, False)

    one_hot = (
        lang_ids[:, None] == jnp.arange(gain_table.shape[0], dtype=jnp.int32)[None, :]
    ).astype(F32)
    token_gains = jnp.dot(one_hot, gain_table, precision=lax.Precision.HIGHEST)
    values = tokens.astype(F32)
    scaled = (values * token_gains).astype(BF)
    squares = jnp.sum(values * values, axis=1, keepdims=True)
    high, low = high_low(squares)
    pad = jnp.zeros((rows, 126), BF)
    block = jnp.concatenate([scaled, high, low, pad], axis=1)
    block = lax.dynamic_slice(
        jnp.concatenate([block, block], axis=0), (z * 8, 0), block.shape
    ).reshape(8, 8, width + 128)

    from_1, from_2, from_3 = (swap_x(block, bits) for bits in (1, 2, 3))
    piece_a0 = swap_x(away_a0, 1)
    from_1, from_2, from_3, piece_a0, away_a1 = tie(from_1, from_2, from_3, piece_a0, away_a1)
    block = jnp.concatenate(
        [
            jnp.concatenate([block, from_2], axis=1),
            jnp.concatenate([from_1, from_3], axis=1),
        ],
        axis=2,
    )
    from_1, from_2, from_3 = (swap_y(block, bits) for bits in (1, 2, 3))
    piece_a1 = swap_x(away_a1, 1)
    from_1, from_2, from_3, piece_a1, away_b = tie(from_1, from_2, from_3, piece_a1, away_b)
    block = jnp.concatenate([block, from_1, from_2, from_3], axis=1)
    from_core = swap_core(block)
    piece_b = swap_x(away_b, 1)
    block = jnp.concatenate([block, from_core], axis=1)
    edge = width + 128
    here = block[:, :, :width].reshape(-1, width)
    there = block[:, :, edge : edge + width].reshape(-1, width)
    everything = jnp.concatenate([here, there], axis=1)
    square_sums = add(
        block[:, :, width],
        block[:, :, width + 1],
        block[:, :, edge + width],
        block[:, :, edge + width + 1],
    )

    weight_a = jnp.concatenate([both(0, part_a, True), piece_a0, piece_a1], axis=0)
    sums_a = (
        jnp.dot(everything, weight_a, preferred_element_type=F32)
        .astype(BF)
        .reshape(8, -1, 2 * part_a)
    )
    weight_b = jnp.concatenate([both(part_a, part_b, True), piece_b], axis=0)
    sums_b = (
        jnp.dot(everything, weight_b, preferred_element_type=F32)
        .astype(BF)
        .reshape(8, -1, 2 * part_b)
    )

    cut = 2 * part_a

    def with_squares(k, arrived=None):
        total = square_sums[k][:, None]
        if arrived is None:
            body = sums_a[k]
        else:
            body = add(sums_a[k], arrived[:, :cut]).astype(BF)
            total = total + add(arrived[:, cut : cut + 1], arrived[:, cut + 1 : cut + 2])
        high, low = high_low(total)
        return jnp.concatenate([body, high, low, jnp.zeros((body.shape[0], 126), BF)], axis=1)

    def pair(send_up, send_down):
        send_up, send_down = tie(send_up, send_down)
        return tie(shift_z(send_up, 1), shift_z(send_down, -1))

    up_a = shift_z(with_squares(4), 1)
    down_b = shift_z(sums_b[4], -1)
    down_a = up_b = None
    for hop in (1, 2, 3):
        up_a, down_a = pair(with_squares(4 - hop, up_a), with_squares(4 + hop, down_a))
        if hop == 1:
            up_a, down_a, down_b = tie(up_a, down_a, down_b)
        else:
            up_a, down_a, up_b, down_b = tie(up_a, down_a, up_b, down_b)
        if hop == 2:
            up_a, down_weight = tie(up_a, down_weight)
        send_up = sums_b[3] if up_b is None else add(sums_b[4 - hop], up_b).astype(BF)
        up_b, down_b = pair(send_up, add(sums_b[4 + hop], down_b).astype(BF))

    all_squares = square_sums[0][:, None] + add(
        up_a[:, cut : cut + 1],
        up_a[:, cut + 1 : cut + 2],
        down_a[:, cut : cut + 1],
        down_a[:, cut + 1 : cut + 2],
    )
    inverse_rms = lax.rsqrt(all_squares / (width * 16) + 1e-05)

    def activate(summed, count):
        gate = summed[:, :count] * inverse_rms
        up = summed[:, count:] * inverse_rms
        return (jax.nn.silu(gate) * up).astype(BF)

    hidden_a = activate(add(sums_a[0], up_a[:, :cut], down_a[:, :cut]), part_a)
    hidden_b = activate(add(sums_b[0], up_b, down_b), part_b)

    down_low, down_high = down_weight[:half], down_weight[half:]
    down_there = swap_x(jnp.where(x_lo == 0, down_high, down_low), 1)
    down_here = jnp.where(x_lo == 0, down_low, down_high)
    down_both = jnp.concatenate([down_here, down_there], axis=1)

    def project(chunks):
        terms = jnp.dot(
            jnp.concatenate(chunks, axis=0), down_both, preferred_element_type=F32
        )
        return terms.astype(BF).reshape(len(chunks), 128, 2 * width)

    def sum_core(terms):
        return add(terms[:, :64], swap_core(terms[:, 64:])).astype(BF)

    def sum_x(terms):
        return add(
            terms[:, :8, :width],
            swap_x(terms[:, :8, width:], 1),
            swap_x(terms[:, 8:, :width], 2),
            swap_x(terms[:, 8:, width:], 3),
        )

    up = down = jnp.concatenate([hidden_a, hidden_b], axis=1)
    chunks = {0: up}
    for step in (1, 2, 3):
        up, down = tie(up, down)
        up, down = shift_z(up, 1), shift_z(down, -1)
        chunks[8 - step], chunks[step] = up, down
    up, down = tie(up[:, :512], down[:, 512:])
    last_up, last_down = shift_z(up, 1), shift_z(down, -1)
    first = sum_core(project([chunks[k] for k in (6, 7, 0, 1, 2)]))
    stay, last_up, last_down = tie(first[:, :16], last_up, last_down)
    first = add(
        stay,
        swap_y(first[:, 16:32], 1),
        swap_y(first[:, 32:48], 2),
        swap_y(first[:, 48:64], 3),
    ).astype(BF)
    chunks[4] = jnp.concatenate([last_up, last_down], axis=1)
    second = project([chunks[k] for k in (3, 4, 5)])
    second = sum_core(second).reshape(3, 4, 2, 8, 2 * width)
    second = add(
        second[:, :, 0, :, :width],
        swap_x(second[:, :, 0, :, width:], 1),
        swap_x(second[:, :, 1, :, :width], 2),
        swap_x(second[:, :, 1, :, width:], 3),
    ).astype(BF)
    second = add(second[:, 0], *(swap_y(second[:, bits], bits) for bits in (1, 2, 3)))
    own_rows = jnp.concatenate([sum_x(first), second], axis=0).reshape(rows, width)
    own_rows = lax.dynamic_slice(
        jnp.concatenate([own_rows, own_rows], axis=0), ((10 - z) % 8 * 8, 0), (rows, width)
    )
    return (values + own_rows).astype(BF)


def solution(mesh):
    return jax.shard_map(
        local,
        mesh=mesh,
        in_specs=(
            P("ffn", "hid"),
            P("ffn"),
            P(None, "hid"),
            P("hid", "ffn"),
            P("hid", "ffn"),
            P("ffn", "hid"),
        ),
        out_specs=P("ffn", "hid"),
        check_vma=False,
    )
```

```python
import jax
import jax.numpy as jnp
from jax import lax
from jax.sharding import PartitionSpec as P

AXES = ("hid", "ffn")
BF = jnp.bfloat16
F32 = jnp.float32


def permutation(move):
    pairs = []
    for xl in range(2):
        for z in range(8):
            for xh in range(2):
                for y in range(4):
                    for core in range(2):
                        x, yy, zz, cc = move(xh * 2 + xl, y, z, core)
                        source = (xl * 8 + z) * 16 + xh * 8 + y * 2 + core
                        target = ((x % 2) * 8 + zz) * 16 + (x // 2) * 8 + yy * 2 + cc
                        pairs.append((source, target))
    return pairs


def swap_x(value, bits):
    return lax.ppermute(value, AXES, permutation(lambda x, y, z, c: (x ^ bits, y, z, c)))


def swap_y(value, bits):
    return lax.ppermute(value, AXES, permutation(lambda x, y, z, c: (x, y ^ bits, z, c)))


def swap_core(value):
    return lax.ppermute(value, AXES, permutation(lambda x, y, z, c: (x, y, z, c ^ 1)))


def shift_z(value, step):
    return lax.ppermute(value, AXES, permutation(lambda x, y, z, c: (x, y, (z + step) % 8, c)))


def tie(*values):
    return lax.optimization_barrier(values)


def add(*terms):
    total = terms[0].astype(F32)
    for term in terms[1:]:
        total = total + term.astype(F32)
    return total


def high_low(value):
    high = value.astype(BF)
    low = (value - high.astype(F32)).astype(BF)
    return high, low


def local(tokens, lang_ids, gain_table, gate_weight, up_weight, down_weight):
    rows, width = tokens.shape
    units = gate_weight.shape[1]
    half = units // 2
    part_a = half - 512
    part_b = half - part_a
    hid = lax.axis_index("hid")
    x_lo, z = hid // 8, hid % 8

    def pick(weight, start, count, mine):
        low = weight[:, start : start + count]
        high = weight[:, half + start : half + start + count]
        return jnp.where((x_lo == 0) == mine, low, high)

    def both(start, count, mine):
        return jnp.concatenate(
            [pick(gate_weight, start, count, mine), pick(up_weight, start, count, mine)], axis=1
        )

    away_a = both(0, part_a, False)
    away_b = both(part_a, part_b, False)

    one_hot = (
        lang_ids[:, None] == jnp.arange(gain_table.shape[0], dtype=jnp.int32)[None, :]
    ).astype(F32)
    token_gains = jnp.dot(one_hot, gain_table, precision=lax.Precision.HIGHEST)
    values = tokens.astype(F32)
    scaled = (values * token_gains).astype(BF)
    squares = jnp.sum(values * values, axis=1, keepdims=True)
    high, low = high_low(squares)
    pad = jnp.zeros((rows, 126), BF)
    block = jnp.concatenate([scaled, high, low, pad], axis=1)
    block = lax.dynamic_slice(
        jnp.concatenate([block, block], axis=0), (z * 8, 0), block.shape
    ).reshape(8, 8, width + 128)

    from_1, from_2, from_3 = (swap_x(block, bits) for bits in (1, 2, 3))
    piece_a0 = swap_x(away_a[:64], 1)
    from_1, from_2, from_3, piece_a0, away_a, away_b = tie(
        from_1, from_2, from_3, piece_a0, away_a, away_b
    )
    block = jnp.concatenate(
        [
            jnp.concatenate([block, from_2], axis=1),
            jnp.concatenate([from_1, from_3], axis=1),
        ],
        axis=2,
    )
    from_1, from_2, from_3 = (swap_y(block, bits) for bits in (1, 2, 3))
    piece_a1 = swap_x(away_a[64:], 1)
    piece_b0 = swap_x(away_b[:192], 1)
    from_1, from_2, from_3, piece_a1, piece_b0, away_b = tie(
        from_1, from_2, from_3, piece_a1, piece_b0, away_b
    )
    block = jnp.concatenate([block, from_1, from_2, from_3], axis=1)
    from_core = swap_core(block)
    piece_b1 = swap_x(away_b[192:], 1)
    block = jnp.concatenate([block, from_core], axis=1)
    edge = width + 128
    here = block[:, :, :width].reshape(-1, width)
    there = block[:, :, edge : edge + width].reshape(-1, width)
    everything = jnp.concatenate([here, there], axis=1)
    square_sums = add(
        block[:, :, width],
        block[:, :, width + 1],
        block[:, :, edge + width],
        block[:, :, edge + width + 1],
    )

    weight_a = jnp.concatenate([both(0, part_a, True), piece_a0, piece_a1], axis=0)
    sums_a = (
        jnp.dot(everything, weight_a, preferred_element_type=F32)
        .astype(BF)
        .reshape(8, -1, 2 * part_a)
    )
    weight_b = jnp.concatenate([both(part_a, part_b, True), piece_b0, piece_b1], axis=0)
    sums_b = (
        jnp.dot(everything, weight_b, preferred_element_type=F32)
        .astype(BF)
        .reshape(8, -1, 2 * part_b)
    )

    cut = 2 * part_a

    def with_squares(k, arrived=None):
        total = square_sums[k][:, None]
        if arrived is None:
            body = sums_a[k]
        else:
            body = add(sums_a[k], arrived[:, :cut]).astype(BF)
            total = total + add(arrived[:, cut : cut + 1], arrived[:, cut + 1 : cut + 2])
        high, low = high_low(total)
        return jnp.concatenate([body, high, low, jnp.zeros((body.shape[0], 126), BF)], axis=1)

    def pair(send_up, send_down):
        send_up, send_down = tie(send_up, send_down)
        return tie(shift_z(send_up, 1), shift_z(send_down, -1))

    up_a = shift_z(with_squares(4), 1)
    down_b = shift_z(sums_b[4], -1)
    down_a = up_b = None
    for hop in (1, 2, 3):
        up_a, down_a = pair(with_squares(4 - hop, up_a), with_squares(4 + hop, down_a))
        if hop == 1:
            up_a, down_a, down_b = tie(up_a, down_a, down_b)
        if hop == 2:
            up_a, down_weight = tie(up_a, down_weight)
        send_up = sums_b[3] if up_b is None else add(sums_b[4 - hop], up_b).astype(BF)
        up_b, down_b = pair(send_up, add(sums_b[4 + hop], down_b).astype(BF))

    all_squares = square_sums[0][:, None] + add(
        up_a[:, cut : cut + 1],
        up_a[:, cut + 1 : cut + 2],
        down_a[:, cut : cut + 1],
        down_a[:, cut + 1 : cut + 2],
    )
    inverse_rms = lax.rsqrt(all_squares / (width * 16) + 1e-05)

    def activate(summed, count):
        gate = summed[:, :count] * inverse_rms
        up = summed[:, count:] * inverse_rms
        return (jax.nn.silu(gate) * up).astype(BF)

    hidden_a = activate(add(sums_a[0], up_a[:, :cut], down_a[:, :cut]), part_a)
    hidden_b = activate(add(sums_b[0], up_b, down_b), part_b)

    down_low, down_high = down_weight[:half], down_weight[half:]
    down_there = swap_x(jnp.where(x_lo == 0, down_high, down_low), 1)
    down_here = jnp.where(x_lo == 0, down_low, down_high)
    down_both = jnp.concatenate([down_here, down_there], axis=1)

    def project(chunks):
        terms = jnp.dot(
            jnp.concatenate(chunks, axis=0), down_both, preferred_element_type=F32
        )
        return terms.astype(BF).reshape(len(chunks), 128, 2 * width)

    def sum_core(terms):
        return add(terms[:, :64], swap_core(terms[:, 64:])).astype(BF)

    def sum_y(terms):
        return add(
            terms[:, :16],
            swap_y(terms[:, 16:32], 1),
            swap_y(terms[:, 32:48], 2),
            swap_y(terms[:, 48:64], 3),
        ).astype(BF)

    def sum_x(terms):
        return add(
            terms[:, :8, :width],
            swap_x(terms[:, :8, width:], 1),
            swap_x(terms[:, 8:, :width], 2),
            swap_x(terms[:, 8:, width:], 3),
        )

    hidden = jnp.concatenate([hidden_a, hidden_b], axis=1)
    chunks = {0: hidden}
    for k, step in ((7, 1), (1, -1), (6, 2), (2, -2)):
        chunks[k] = shift_z(hidden, step)
    below, above = tie(chunks[6], chunks[2])
    chunks[5] = shift_z(below, 1)
    chunks[3] = shift_z(above, -1)
    last = shift_z(above[:, :512], -2), shift_z(below[:, 512:], 2)
    first = sum_core(project([chunks[k] for k in (6, 7, 0, 1, 2)]))
    near = swap_y(first[:, 16:32], 1)
    chunks[4] = jnp.concatenate(last, axis=1)
    second = project([chunks[k] for k in (3, 4, 5)])
    near, second = tie(near, second)
    first = add(
        first[:, :16], near, swap_y(first[:, 32:48], 2), swap_y(first[:, 48:64], 3)
    ).astype(BF)
    second = sum_y(sum_core(second))
    own_rows = jnp.concatenate([sum_x(first), sum_x(second)], axis=0).reshape(rows, width)
    own_rows = lax.dynamic_slice(
        jnp.concatenate([own_rows, own_rows], axis=0), ((10 - z) % 8 * 8, 0), (rows, width)
    )
    return (values + own_rows).astype(BF)


def solution(mesh):
    return jax.shard_map(
        local,
        mesh=mesh,
        in_specs=(
            P("ffn", "hid"),
            P("ffn"),
            P(None, "hid"),
            P("hid", "ffn"),
            P("hid", "ffn"),
            P("ffn", "hid"),
        ),
        out_specs=P("ffn", "hid"),
        check_vma=False,
    )
```

```python
import jax
import jax.numpy as jnp
from jax import lax
from jax.sharding import PartitionSpec as P

AXES = ("hid", "ffn")
BF = jnp.bfloat16
F32 = jnp.float32


def permutation(move):
    pairs = []
    for xl in range(2):
        for z in range(8):
            for xh in range(2):
                for y in range(4):
                    for core in range(2):
                        x, yy, zz, cc = move(xh * 2 + xl, y, z, core)
                        source = (xl * 8 + z) * 16 + xh * 8 + y * 2 + core
                        target = ((x % 2) * 8 + zz) * 16 + (x // 2) * 8 + yy * 2 + cc
                        pairs.append((source, target))
    return pairs


def swap_x(value, bits):
    return lax.ppermute(value, AXES, permutation(lambda x, y, z, c: (x ^ bits, y, z, c)))


def swap_y(value, bits):
    return lax.ppermute(value, AXES, permutation(lambda x, y, z, c: (x, y ^ bits, z, c)))


def swap_core(value):
    return lax.ppermute(value, AXES, permutation(lambda x, y, z, c: (x, y, z, c ^ 1)))


def shift_z(value, step):
    return lax.ppermute(value, AXES, permutation(lambda x, y, z, c: (x, y, (z + step) % 8, c)))


def tie(*values):
    return lax.optimization_barrier(values)


def add(*terms):
    total = terms[0].astype(F32)
    for term in terms[1:]:
        total = total + term.astype(F32)
    return total


def high_low(value):
    high = value.astype(BF)
    low = (value - high.astype(F32)).astype(BF)
    return high, low


def local(tokens, lang_ids, gain_table, gate_weight, up_weight, down_weight):
    rows, width = tokens.shape
    units = gate_weight.shape[1]
    half = units // 2
    part_a = 512
    part_b = half - part_a
    hid = lax.axis_index("hid")
    x_lo, z = hid // 8, hid % 8

    def pick(weight, start, count, mine):
        low = weight[:, start : start + count]
        high = weight[:, half + start : half + start + count]
        return jnp.where((x_lo == 0) == mine, low, high)

    def both(start, count, mine):
        return jnp.concatenate(
            [pick(gate_weight, start, count, mine), pick(up_weight, start, count, mine)], axis=1
        )

    away_a = both(0, part_a, False)
    away_b = both(part_a, part_b, False)

    one_hot = (
        lang_ids[:, None] == jnp.arange(gain_table.shape[0], dtype=jnp.int32)[None, :]
    ).astype(F32)
    token_gains = jnp.dot(one_hot, gain_table, precision=lax.Precision.HIGHEST)
    values = tokens.astype(F32)
    scaled = (values * token_gains).astype(BF)
    squares = jnp.sum(values * values, axis=1, keepdims=True)
    high, low = high_low(squares)
    pad = jnp.zeros((rows, 126), BF)
    block = jnp.concatenate([scaled, high, low, pad], axis=1)
    block = lax.dynamic_slice(
        jnp.concatenate([block, block], axis=0), (z * 8, 0), block.shape
    ).reshape(8, 8, width + 128)

    from_1, from_2, from_3 = (swap_x(block, bits) for bits in (1, 2, 3))
    piece_a0 = swap_x(away_a[:64], 1)
    from_1, from_2, from_3, piece_a0, away_a, away_b = tie(
        from_1, from_2, from_3, piece_a0, away_a, away_b
    )
    block = jnp.concatenate(
        [
            jnp.concatenate([block, from_2], axis=1),
            jnp.concatenate([from_1, from_3], axis=1),
        ],
        axis=2,
    )
    from_1, from_2, from_3 = (swap_y(block, bits) for bits in (1, 2, 3))
    piece_a1 = swap_x(away_a[64:], 1)
    piece_b0 = swap_x(away_b[:96], 1)
    from_1, from_2, from_3, piece_a1, piece_b0, away_b = tie(
        from_1, from_2, from_3, piece_a1, piece_b0, away_b
    )
    block = jnp.concatenate([block, from_1, from_2, from_3], axis=1)
    from_core = swap_core(block)
    piece_b1 = swap_x(away_b[96:], 1)
    block = jnp.concatenate([block, from_core], axis=1)
    edge = width + 128
    here = block[:, :, :width].reshape(-1, width)
    there = block[:, :, edge : edge + width].reshape(-1, width)
    everything = jnp.concatenate([here, there], axis=1)
    square_sums = add(
        block[:, :, width],
        block[:, :, width + 1],
        block[:, :, edge + width],
        block[:, :, edge + width + 1],
    )

    weight_a = jnp.concatenate([both(0, part_a, True), piece_a0, piece_a1], axis=0)
    sums_a = (
        jnp.dot(everything, weight_a, preferred_element_type=F32)
        .astype(BF)
        .reshape(8, -1, 2 * part_a)
    )
    up_a = shift_z(sums_a[4], 1)
    up_a, piece_b1 = tie(up_a, piece_b1)
    weight_b = jnp.concatenate([both(part_a, part_b, True), piece_b0, piece_b1], axis=0)
    sums_b = (
        jnp.dot(everything, weight_b, preferred_element_type=F32)
        .astype(BF)
        .reshape(8, -1, 2 * part_b)
    )

    cut = 2 * part_b

    def with_squares(k, arrived=None):
        total = square_sums[k][:, None]
        if arrived is None:
            body = sums_b[k]
        else:
            body = add(sums_b[k], arrived[:, :cut]).astype(BF)
            total = total + add(arrived[:, cut : cut + 1], arrived[:, cut + 1 : cut + 2])
        high, low = high_low(total)
        return jnp.concatenate([body, high, low, jnp.zeros((body.shape[0], 126), BF)], axis=1)

    def pair(send_up, send_down):
        send_up, send_down = tie(send_up, send_down)
        return tie(shift_z(send_up, 1), shift_z(send_down, -1))

    down_b = shift_z(with_squares(4), -1)
    down_a = up_b = None
    for hop in (1, 2, 3):
        send_down = sums_a[5] if down_a is None else add(sums_a[4 + hop], down_a).astype(BF)
        up_a, down_a = pair(add(sums_a[4 - hop], up_a).astype(BF), send_down)
        if hop == 2:
            up_a, down_weight = tie(up_a, down_weight)
        up_b, down_b = pair(with_squares(4 - hop, up_b), with_squares(4 + hop, down_b))

    all_squares = square_sums[0][:, None] + add(
        up_b[:, cut : cut + 1],
        up_b[:, cut + 1 : cut + 2],
        down_b[:, cut : cut + 1],
        down_b[:, cut + 1 : cut + 2],
    )
    inverse_rms = lax.rsqrt(all_squares / (width * 16) + 1e-05)

    def activate(summed, count):
        gate = summed[:, :count] * inverse_rms
        up = summed[:, count:] * inverse_rms
        return (jax.nn.silu(gate) * up).astype(BF)

    hidden_a = activate(add(sums_a[0], up_a, down_a), part_a)
    hidden_b = activate(add(sums_b[0], up_b[:, :cut], down_b[:, :cut]), part_b)

    down_low, down_high = down_weight[:half], down_weight[half:]
    down_there = swap_x(jnp.where(x_lo == 0, down_high, down_low), 1)
    down_here = jnp.where(x_lo == 0, down_low, down_high)
    down_both = jnp.concatenate([down_here, down_there], axis=1)

    def project(chunks):
        terms = jnp.dot(
            jnp.concatenate(chunks, axis=0), down_both, preferred_element_type=F32
        )
        return terms.astype(BF).reshape(len(chunks), 128, 2 * width)

    def sum_core(terms):
        return add(terms[:, :64], swap_core(terms[:, 64:])).astype(BF)

    def sum_y(terms):
        return add(
            terms[:, :16],
            swap_y(terms[:, 16:32], 1),
            swap_y(terms[:, 32:48], 2),
            swap_y(terms[:, 48:64], 3),
        ).astype(BF)

    def sum_x(terms):
        return add(
            terms[:, :8, :width],
            swap_x(terms[:, :8, width:], 1),
            swap_x(terms[:, 8:, :width], 2),
            swap_x(terms[:, 8:, width:], 3),
        )

    hidden = jnp.concatenate([hidden_a, hidden_b], axis=1)
    chunks = {0: hidden}
    for k, step in ((7, 1), (1, -1), (6, 2), (2, -2)):
        chunks[k] = shift_z(hidden, step)
    below, above = tie(chunks[6], chunks[2])
    chunks[5] = shift_z(below, 1)
    chunks[3] = shift_z(above, -1)
    last = shift_z(above[:, :512], -2), shift_z(below[:, 512:], 2)
    first = sum_core(project([chunks[k] for k in (6, 7, 0, 1, 2)]))
    near = swap_y(first[:, 16:32], 1)
    chunks[4] = jnp.concatenate(last, axis=1)
    second = project([chunks[k] for k in (3, 4, 5)])
    near, second = tie(near, second)
    first = add(
        first[:, :16], near, swap_y(first[:, 32:48], 2), swap_y(first[:, 48:64], 3)
    ).astype(BF)
    second = sum_y(sum_core(second))
    own_rows = jnp.concatenate([sum_x(first), sum_x(second)], axis=0).reshape(rows, width)
    own_rows = lax.dynamic_slice(
        jnp.concatenate([own_rows, own_rows], axis=0), ((10 - z) % 8 * 8, 0), (rows, width)
    )
    return (values + own_rows).astype(BF)


def solution(mesh):
    return jax.shard_map(
        local,
        mesh=mesh,
        in_specs=(
            P("ffn", "hid"),
            P("ffn"),
            P(None, "hid"),
            P("hid", "ffn"),
            P("hid", "ffn"),
            P("ffn", "hid"),
        ),
        out_specs=P("ffn", "hid"),
        check_vma=False,
    )
```

```python
import jax
import jax.numpy as jnp
from jax import lax
from jax.sharding import PartitionSpec as P

AXES = ("hid", "ffn")
BF = jnp.bfloat16
F32 = jnp.float32


def permutation(move):
    pairs = []
    for xl in range(2):
        for z in range(8):
            for xh in range(2):
                for y in range(4):
                    for core in range(2):
                        x, yy, zz, cc = move(xh * 2 + xl, y, z, core)
                        source = (xl * 8 + z) * 16 + xh * 8 + y * 2 + core
                        target = ((x % 2) * 8 + zz) * 16 + (x // 2) * 8 + yy * 2 + cc
                        pairs.append((source, target))
    return pairs


def swap_x(value, bits):
    return lax.ppermute(value, AXES, permutation(lambda x, y, z, c: (x ^ bits, y, z, c)))


def swap_y(value, bits):
    return lax.ppermute(value, AXES, permutation(lambda x, y, z, c: (x, y ^ bits, z, c)))


def swap_core(value):
    return lax.ppermute(value, AXES, permutation(lambda x, y, z, c: (x, y, z, c ^ 1)))


def shift_z(value, step):
    return lax.ppermute(value, AXES, permutation(lambda x, y, z, c: (x, y, (z + step) % 8, c)))


def tie(*values):
    return lax.optimization_barrier(values)


def add(*terms):
    total = terms[0].astype(F32)
    for term in terms[1:]:
        total = total + term.astype(F32)
    return total


def high_low(value):
    high = value.astype(BF)
    low = (value - high.astype(F32)).astype(BF)
    return high, low


def local(tokens, lang_ids, gain_table, gate_weight, up_weight, down_weight):
    rows, width = tokens.shape
    units = gate_weight.shape[1]
    half = units // 2
    part_a = 512
    part_b = half - part_a
    hid = lax.axis_index("hid")
    x_lo, z = hid // 8, hid % 8

    def pick(weight, start, count, mine):
        low = weight[:, start : start + count]
        high = weight[:, half + start : half + start + count]
        return jnp.where((x_lo == 0) == mine, low, high)

    def both(start, count, mine):
        return jnp.concatenate(
            [pick(gate_weight, start, count, mine), pick(up_weight, start, count, mine)], axis=1
        )

    away_a = both(0, part_a, False)
    away_b = both(part_a, part_b, False)

    one_hot = (
        lang_ids[:, None] == jnp.arange(gain_table.shape[0], dtype=jnp.int32)[None, :]
    ).astype(F32)
    token_gains = jnp.dot(one_hot, gain_table, precision=lax.Precision.HIGHEST)
    values = tokens.astype(F32)
    scaled = (values * token_gains).astype(BF)
    squares = jnp.sum(values * values, axis=1, keepdims=True)
    high, low = high_low(squares)
    pad = jnp.zeros((rows, 126), BF)
    block = jnp.concatenate([scaled, high, low, pad], axis=1)
    block = lax.dynamic_slice(
        jnp.concatenate([block, block], axis=0), (z * 8, 0), block.shape
    ).reshape(8, 8, width + 128)

    from_1, from_2, from_3 = (swap_x(block, bits) for bits in (1, 2, 3))
    piece_a0 = swap_x(away_a[:64], 1)
    from_1, from_2, from_3, piece_a0, away_a, away_b = tie(
        from_1, from_2, from_3, piece_a0, away_a, away_b
    )
    block = jnp.concatenate(
        [
            jnp.concatenate([block, from_2], axis=1),
            jnp.concatenate([from_1, from_3], axis=1),
        ],
        axis=2,
    )
    from_1, from_2, from_3 = (swap_y(block, bits) for bits in (1, 2, 3))
    piece_a1 = swap_x(away_a[64:], 1)
    piece_b0 = swap_x(away_b[:96], 1)
    from_1, from_2, from_3, piece_a1, piece_b0, away_b = tie(
        from_1, from_2, from_3, piece_a1, piece_b0, away_b
    )
    block = jnp.concatenate([block, from_1, from_2, from_3], axis=1)
    from_core = swap_core(block)
    piece_b1 = swap_x(away_b[96:], 1)
    block = jnp.concatenate([block, from_core], axis=1)
    edge = width + 128
    here = block[:, :, :width].reshape(-1, width)
    there = block[:, :, edge : edge + width].reshape(-1, width)
    everything = jnp.concatenate([here, there], axis=1)
    square_sums = add(
        block[:, :, width],
        block[:, :, width + 1],
        block[:, :, edge + width],
        block[:, :, edge + width + 1],
    )

    weight_a = jnp.concatenate([both(0, part_a, True), piece_a0, piece_a1], axis=0)
    sums_a = (
        jnp.dot(everything, weight_a, preferred_element_type=F32)
        .astype(BF)
        .reshape(8, -1, 2 * part_a)
    )
    up_a = shift_z(sums_a[4], 1)
    up_a, piece_b1 = tie(up_a, piece_b1)
    weight_b = jnp.concatenate([both(part_a, part_b, True), piece_b0, piece_b1], axis=0)
    sums_b = (
        jnp.dot(everything, weight_b, preferred_element_type=F32)
        .astype(BF)
        .reshape(8, -1, 2 * part_b)
    )

    cut = 2 * part_b

    def with_squares(k, arrived=None):
        total = square_sums[k][:, None]
        if arrived is None:
            body = sums_b[k]
        else:
            body = add(sums_b[k], arrived[:, :cut]).astype(BF)
            total = total + add(arrived[:, cut : cut + 1], arrived[:, cut + 1 : cut + 2])
        high, low = high_low(total)
        return jnp.concatenate([body, high, low, jnp.zeros((body.shape[0], 126), BF)], axis=1)

    def pair(send_up, send_down):
        send_up, send_down = tie(send_up, send_down)
        return tie(shift_z(send_up, 1), shift_z(send_down, -1))

    down_b = shift_z(with_squares(4), -1)
    down_a = up_b = None
    for hop in (1, 2, 3):
        send_down = sums_a[5] if down_a is None else add(sums_a[4 + hop], down_a).astype(BF)
        up_a, down_a = pair(add(sums_a[4 - hop], up_a).astype(BF), send_down)
        if hop == 2:
            up_a, down_weight = tie(up_a, down_weight)
        up_b, down_b = pair(with_squares(4 - hop, up_b), with_squares(4 + hop, down_b))

    all_squares = square_sums[0][:, None] + add(
        up_b[:, cut : cut + 1],
        up_b[:, cut + 1 : cut + 2],
        down_b[:, cut : cut + 1],
        down_b[:, cut + 1 : cut + 2],
    )
    inverse_rms = lax.rsqrt(all_squares / (width * 16) + 1e-05)

    def activate(summed, count):
        gate = summed[:, :count] * inverse_rms
        up = summed[:, count:] * inverse_rms
        return (jax.nn.silu(gate) * up).astype(BF)

    hidden_a = activate(add(sums_a[0], up_a, down_a), part_a)
    hidden_b = activate(add(sums_b[0], up_b[:, :cut], down_b[:, :cut]), part_b)

    down_low, down_high = down_weight[:half], down_weight[half:]
    down_there = swap_x(jnp.where(x_lo == 0, down_high, down_low), 1)
    down_here = jnp.where(x_lo == 0, down_low, down_high)
    down_both = jnp.concatenate([down_here, down_there], axis=1)

    def project(chunks):
        terms = jnp.dot(
            jnp.concatenate([jnp.concatenate(chunk, axis=1) for chunk in chunks], axis=0),
            down_both,
            preferred_element_type=F32,
        )
        return terms.astype(BF).reshape(len(chunks), 128, 2 * width)

    def sum_core(terms):
        return add(terms[:, :64], swap_core(terms[:, 64:])).astype(BF)

    chunks = {0: (hidden_a, hidden_b)}
    up = down = chunks[0]
    for step in (1, 2, 3):
        up = (shift_z(up[0], 1), shift_z(up[1], 1))
        down = (shift_z(down[0], -1), shift_z(down[1], -1))
        chunks[8 - step], chunks[step] = up, down
    chunks[4] = (shift_z(up[0], 1), shift_z(down[1], -1))
    first = sum_core(project([chunks[k] for k in (6, 7, 0, 1, 2)]))
    second = sum_core(project([chunks[k] for k in (3, 4, 5)]))
    terms = jnp.concatenate([first, second], axis=0)
    terms = add(
        terms[:, :16], *(swap_y(terms[:, 16 * bits : 16 * bits + 16], bits) for bits in (1, 2, 3))
    ).astype(BF)
    own_rows = add(
        terms[:, :8, :width],
        swap_x(terms[:, :8, width:], 1),
        swap_x(terms[:, 8:, :width], 2),
        swap_x(terms[:, 8:, width:], 3),
    ).reshape(rows, width)
    own_rows = lax.dynamic_slice(
        jnp.concatenate([own_rows, own_rows], axis=0), ((10 - z) % 8 * 8, 0), (rows, width)
    )
    return (values + own_rows).astype(BF)


def solution(mesh):
    return jax.shard_map(
        local,
        mesh=mesh,
        in_specs=(
            P("ffn", "hid"),
            P("ffn"),
            P(None, "hid"),
            P("hid", "ffn"),
            P("hid", "ffn"),
            P("ffn", "hid"),
        ),
        out_specs=P("ffn", "hid"),
        check_vma=False,
    )
```

```python
import jax
import jax.numpy as jnp
from jax import lax
from jax.sharding import PartitionSpec as P

AXES = ("hid", "ffn")
BF = jnp.bfloat16
F32 = jnp.float32


def permutation(move):
    pairs = []
    for xl in range(2):
        for z in range(8):
            for xh in range(2):
                for y in range(4):
                    for core in range(2):
                        x, yy, zz, cc = move(xh * 2 + xl, y, z, core)
                        source = (xl * 8 + z) * 16 + xh * 8 + y * 2 + core
                        target = ((x % 2) * 8 + zz) * 16 + (x // 2) * 8 + yy * 2 + cc
                        pairs.append((source, target))
    return pairs


def swap_x(value, bits):
    return lax.ppermute(value, AXES, permutation(lambda x, y, z, c: (x ^ bits, y, z, c)))


def swap_y(value, bits):
    return lax.ppermute(value, AXES, permutation(lambda x, y, z, c: (x, y ^ bits, z, c)))


def swap_core(value):
    return lax.ppermute(value, AXES, permutation(lambda x, y, z, c: (x, y, z, c ^ 1)))


def shift_z(value, step):
    return lax.ppermute(value, AXES, permutation(lambda x, y, z, c: (x, y, (z + step) % 8, c)))


def tie(*values):
    return lax.optimization_barrier(values)


def add(*terms):
    total = terms[0].astype(F32)
    for term in terms[1:]:
        total = total + term.astype(F32)
    return total


def high_low(value):
    high = value.astype(BF)
    low = (value - high.astype(F32)).astype(BF)
    return high, low


def local(tokens, lang_ids, gain_table, gate_weight, up_weight, down_weight):
    rows, width = tokens.shape
    units = gate_weight.shape[1]
    half = units // 2
    part_a = 512
    part_b = half - part_a
    hid = lax.axis_index("hid")
    x_lo, z = hid // 8, hid % 8

    def pick(weight, start, count, mine):
        low = weight[:, start : start + count]
        high = weight[:, half + start : half + start + count]
        return jnp.where((x_lo == 0) == mine, low, high)

    def both(start, count, mine):
        return jnp.concatenate(
            [pick(gate_weight, start, count, mine), pick(up_weight, start, count, mine)], axis=1
        )

    away_a = both(0, part_a, False)
    away_b = both(part_a, part_b, False)

    one_hot = (
        lang_ids[:, None] == jnp.arange(gain_table.shape[0], dtype=jnp.int32)[None, :]
    ).astype(F32)
    token_gains = jnp.dot(one_hot, gain_table, precision=lax.Precision.HIGHEST)
    values = tokens.astype(F32)
    scaled = (values * token_gains).astype(BF)
    squares = jnp.sum(values * values, axis=1, keepdims=True)
    high, low = high_low(squares)
    pad = jnp.zeros((rows, 126), BF)
    block = jnp.concatenate([scaled, high, low, pad], axis=1)
    block = lax.dynamic_slice(
        jnp.concatenate([block, block], axis=0), (z * 8, 0), block.shape
    ).reshape(8, 8, width + 128)

    from_1, from_2, from_3 = (swap_x(block, bits) for bits in (1, 2, 3))
    piece_a0 = swap_x(away_a[:128], 1)
    from_1, from_2, from_3, piece_a0, away_a, away_b = tie(
        from_1, from_2, from_3, piece_a0, away_a, away_b
    )
    block = jnp.concatenate(
        [
            jnp.concatenate([block, from_2], axis=1),
            jnp.concatenate([from_1, from_3], axis=1),
        ],
        axis=2,
    )
    from_1, from_2, from_3 = (swap_y(block, bits) for bits in (1, 2, 3))
    piece_a1 = swap_x(away_a[128:], 1)
    piece_b0 = swap_x(away_b[:176], 1)
    from_1, from_2, from_3, piece_a1, piece_b0, away_b = tie(
        from_1, from_2, from_3, piece_a1, piece_b0, away_b
    )
    block = jnp.concatenate([block, from_1, from_2, from_3], axis=1)
    from_core = swap_core(block)
    piece_b1 = swap_x(away_b[176:], 1)
    block = jnp.concatenate([block, from_core], axis=1)
    edge = width + 128
    here = block[:, :, :width].reshape(-1, width)
    there = block[:, :, edge : edge + width].reshape(-1, width)
    everything = jnp.concatenate([here, there], axis=1)
    square_sums = add(
        block[:, :, width],
        block[:, :, width + 1],
        block[:, :, edge + width],
        block[:, :, edge + width + 1],
    )

    weight_a = jnp.concatenate([both(0, part_a, True), piece_a0, piece_a1], axis=0)
    sums_a = (
        jnp.dot(everything, weight_a, preferred_element_type=F32)
        .astype(BF)
        .reshape(8, -1, 2 * part_a)
    )
    up_a = shift_z(sums_a[4], 1)
    up_a, piece_b1 = tie(up_a, piece_b1)
    weight_b = jnp.concatenate([both(part_a, part_b, True), piece_b0, piece_b1], axis=0)
    sums_b = (
        jnp.dot(everything, weight_b, preferred_element_type=F32)
        .astype(BF)
        .reshape(8, -1, 2 * part_b)
    )

    cut = 2 * part_b

    def with_squares(k, arrived=None):
        total = square_sums[k][:, None]
        if arrived is None:
            body = sums_b[k]
        else:
            body = add(sums_b[k], arrived[:, :cut]).astype(BF)
            total = total + add(arrived[:, cut : cut + 1], arrived[:, cut + 1 : cut + 2])
        high, low = high_low(total)
        return jnp.concatenate([body, high, low, jnp.zeros((body.shape[0], 126), BF)], axis=1)

    def pair(send_up, send_down):
        send_up, send_down = tie(send_up, send_down)
        return tie(shift_z(send_up, 1), shift_z(send_down, -1))

    down_b = shift_z(with_squares(4), -1)
    down_a = up_b = None
    for hop in (1, 2, 3):
        send_down = sums_a[5] if down_a is None else add(sums_a[4 + hop], down_a).astype(BF)
        up_a, down_a = pair(add(sums_a[4 - hop], up_a).astype(BF), send_down)
        if hop == 2:
            up_a, down_weight = tie(up_a, down_weight)
        up_b, down_b = pair(with_squares(4 - hop, up_b), with_squares(4 + hop, down_b))

    all_squares = square_sums[0][:, None] + add(
        up_b[:, cut : cut + 1],
        up_b[:, cut + 1 : cut + 2],
        down_b[:, cut : cut + 1],
        down_b[:, cut + 1 : cut + 2],
    )
    inverse_rms = lax.rsqrt(all_squares / (width * 16) + 1e-05)

    def activate(summed, count):
        gate = summed[:, :count] * inverse_rms
        up = summed[:, count:] * inverse_rms
        return (jax.nn.silu(gate) * up).astype(BF)

    hidden_a = activate(add(sums_a[0], up_a, down_a), part_a)
    hidden_b = activate(add(sums_b[0], up_b[:, :cut], down_b[:, :cut]), part_b)

    down_low, down_high = down_weight[:half], down_weight[half:]
    down_there = swap_x(jnp.where(x_lo == 0, down_high, down_low), 1)
    down_here = jnp.where(x_lo == 0, down_low, down_high)
    down_both = jnp.concatenate([down_here, down_there], axis=1)

    def project(chunks):
        terms = jnp.dot(
            jnp.concatenate([jnp.concatenate(chunk, axis=1) for chunk in chunks], axis=0),
            down_both,
            preferred_element_type=F32,
        )
        return terms.astype(BF).reshape(len(chunks), 128, 2 * width)

    def sum_core(terms):
        return add(terms[:, :64], swap_core(terms[:, 64:])).astype(BF)

    chunks = {0: (hidden_a, hidden_b)}
    up = down = chunks[0]
    for step in (1, 2, 3):
        up = (shift_z(up[0], 1), shift_z(up[1], 1))
        down = (shift_z(down[0], -1), shift_z(down[1], -1))
        chunks[8 - step], chunks[step] = up, down
    chunks[4] = (shift_z(up[0], 1), shift_z(down[1], -1))
    first = sum_core(project([chunks[k] for k in (6, 7, 0, 1, 2)]))
    second = sum_core(project([chunks[k] for k in (3, 4, 5)]))
    terms = jnp.concatenate([first, second], axis=0)
    terms = add(
        terms[:, :16], *(swap_y(terms[:, 16 * bits : 16 * bits + 16], bits) for bits in (1, 2, 3))
    ).astype(BF)
    own_rows = add(
        terms[:, :8, :width],
        swap_x(terms[:, :8, width:], 1),
        swap_x(terms[:, 8:, :width], 2),
        swap_x(terms[:, 8:, width:], 3),
    ).reshape(rows, width)
    own_rows = lax.dynamic_slice(
        jnp.concatenate([own_rows, own_rows], axis=0), ((10 - z) % 8 * 8, 0), (rows, width)
    )
    return (values + own_rows).astype(BF)


def solution(mesh):
    return jax.shard_map(
        local,
        mesh=mesh,
        in_specs=(
            P("ffn", "hid"),
            P("ffn"),
            P(None, "hid"),
            P("hid", "ffn"),
            P("hid", "ffn"),
            P("ffn", "hid"),
        ),
        out_specs=P("ffn", "hid"),
        check_vma=False,
    )
```

```python
import jax
import jax.numpy as jnp
from jax import lax
from jax.sharding import PartitionSpec as P

AXES = ("hid", "ffn")
BF = jnp.bfloat16
F32 = jnp.float32


def permutation(move):
    pairs = []
    for xl in range(2):
        for z in range(8):
            for xh in range(2):
                for y in range(4):
                    for core in range(2):
                        x, yy, zz, cc = move(xh * 2 + xl, y, z, core)
                        source = (xl * 8 + z) * 16 + xh * 8 + y * 2 + core
                        target = ((x % 2) * 8 + zz) * 16 + (x // 2) * 8 + yy * 2 + cc
                        pairs.append((source, target))
    return pairs


def swap_x(value, bits):
    return lax.ppermute(value, AXES, permutation(lambda x, y, z, c: (x ^ bits, y, z, c)))


def swap_y(value, bits):
    return lax.ppermute(value, AXES, permutation(lambda x, y, z, c: (x, y ^ bits, z, c)))


def swap_core(value):
    return lax.ppermute(value, AXES, permutation(lambda x, y, z, c: (x, y, z, c ^ 1)))


def shift_z(value, step):
    return lax.ppermute(value, AXES, permutation(lambda x, y, z, c: (x, y, (z + step) % 8, c)))


def tie(*values):
    return lax.optimization_barrier(values)


def add(*terms):
    total = terms[0].astype(F32)
    for term in terms[1:]:
        total = total + term.astype(F32)
    return total


def high_low(value):
    high = value.astype(BF)
    low = (value - high.astype(F32)).astype(BF)
    return high, low


def local(tokens, lang_ids, gain_table, gate_weight, up_weight, down_weight):
    rows, width = tokens.shape
    units = gate_weight.shape[1]
    half = units // 2
    part_a = 512
    part_b = half - part_a
    hid = lax.axis_index("hid")
    x_lo, z = hid // 8, hid % 8

    def pick(weight, start, count, mine):
        low = weight[:, start : start + count]
        high = weight[:, half + start : half + start + count]
        return jnp.where((x_lo == 0) == mine, low, high)

    def both(start, count, mine):
        return jnp.concatenate(
            [pick(gate_weight, start, count, mine), pick(up_weight, start, count, mine)], axis=1
        )

    away_a = both(0, part_a, False)
    away_b = both(part_a, part_b, False)

    one_hot = (
        lang_ids[:, None] == jnp.arange(gain_table.shape[0], dtype=jnp.int32)[None, :]
    ).astype(F32)
    token_gains = jnp.dot(one_hot, gain_table, precision=lax.Precision.HIGHEST)
    values = tokens.astype(F32)
    scaled = (values * token_gains).astype(BF)
    squares = jnp.sum(values * values, axis=1, keepdims=True)
    high, low = high_low(squares)
    pad = jnp.zeros((rows, 126), BF)
    block = jnp.concatenate([scaled, high, low, pad], axis=1)
    block = lax.dynamic_slice(
        jnp.concatenate([block, block], axis=0), (z * 8, 0), block.shape
    ).reshape(8, 8, width + 128)

    from_1, from_2, from_3 = (swap_x(block, bits) for bits in (1, 2, 3))
    piece_a0 = swap_x(away_a[:64], 1)
    from_1, from_2, from_3, piece_a0, away_a, away_b = tie(
        from_1, from_2, from_3, piece_a0, away_a, away_b
    )
    block = jnp.concatenate(
        [
            jnp.concatenate([block, from_2], axis=1),
            jnp.concatenate([from_1, from_3], axis=1),
        ],
        axis=2,
    )
    from_1, from_2, from_3 = (swap_y(block, bits) for bits in (1, 2, 3))
    piece_a1 = swap_x(away_a[64:], 1)
    piece_b0 = swap_x(away_b[:96], 1)
    from_1, from_2, from_3, piece_a1, piece_b0, away_b = tie(
        from_1, from_2, from_3, piece_a1, piece_b0, away_b
    )
    block = jnp.concatenate([block, from_1, from_2, from_3], axis=1)
    from_core = swap_core(block)
    piece_b1 = swap_x(away_b[96:], 1)
    block = jnp.concatenate([block, from_core], axis=1)
    edge = width + 128
    here = block[:, :, :width].reshape(-1, width)
    there = block[:, :, edge : edge + width].reshape(-1, width)
    everything = jnp.concatenate([here, there], axis=1)
    square_sums = add(
        block[:, :, width],
        block[:, :, width + 1],
        block[:, :, edge + width],
        block[:, :, edge + width + 1],
    )

    weight_a = jnp.concatenate([both(0, part_a, True), piece_a0, piece_a1], axis=0)
    sums_a = (
        jnp.dot(everything, weight_a, preferred_element_type=F32)
        .astype(BF)
        .reshape(8, -1, 2 * part_a)
    )
    up_a = shift_z(sums_a[4], 1)
    up_a, piece_b1 = tie(up_a, piece_b1)
    weight_b = jnp.concatenate([both(part_a, part_b, True), piece_b0, piece_b1], axis=0)
    sums_b = (
        jnp.dot(everything, weight_b, preferred_element_type=F32)
        .astype(BF)
        .reshape(8, -1, 2 * part_b)
    )

    cut = 2 * part_b

    def with_squares(k, arrived=None):
        total = square_sums[k][:, None]
        if arrived is None:
            body = sums_b[k]
        else:
            body = add(sums_b[k], arrived[:, :cut]).astype(BF)
            total = total + add(arrived[:, cut : cut + 1], arrived[:, cut + 1 : cut + 2])
        high, low = high_low(total)
        return jnp.concatenate([body, high, low, jnp.zeros((body.shape[0], 126), BF)], axis=1)

    def pair(send_up, send_down):
        send_up, send_down = tie(send_up, send_down)
        return tie(shift_z(send_up, 1), shift_z(send_down, -1))

    down_b = shift_z(with_squares(4), -1)
    down_a = up_b = None
    for hop in (1, 2, 3):
        send_down = sums_a[5] if down_a is None else add(sums_a[4 + hop], down_a).astype(BF)
        up_a, down_a = pair(add(sums_a[4 - hop], up_a).astype(BF), send_down)
        if hop == 2:
            up_a, down_weight = tie(up_a, down_weight)
        up_b, down_b = pair(with_squares(4 - hop, up_b), with_squares(4 + hop, down_b))

    all_squares = square_sums[0][:, None] + add(
        up_b[:, cut : cut + 1],
        up_b[:, cut + 1 : cut + 2],
        down_b[:, cut : cut + 1],
        down_b[:, cut + 1 : cut + 2],
    )
    inverse_rms = lax.rsqrt(all_squares / (width * 16) + 1e-05)

    def activate(summed, count):
        gate = summed[:, :count] * inverse_rms
        up = summed[:, count:] * inverse_rms
        return (jax.nn.silu(gate) * up).astype(BF)

    hidden_a = activate(add(sums_a[0], up_a, down_a), part_a)
    hidden_b = activate(add(sums_b[0], up_b[:, :cut], down_b[:, :cut]), part_b)

    down_low, down_high = down_weight[:half], down_weight[half:]
    down_there = swap_x(jnp.where(x_lo == 0, down_high, down_low), 1)
    down_here = jnp.where(x_lo == 0, down_low, down_high)
    down_both = jnp.concatenate([down_here, down_there], axis=1)

    def project(chunks):
        terms = jnp.dot(
            jnp.concatenate([jnp.concatenate(chunk, axis=1) for chunk in chunks], axis=0),
            down_both,
            preferred_element_type=F32,
        )
        return terms.astype(BF).reshape(len(chunks), 128, 2 * width)

    def sum_core(terms):
        return add(terms[:, :64], swap_core(terms[:, 64:])).astype(BF)

    chunks = {0: (hidden_a, hidden_b)}
    up = down = chunks[0]
    for step in (1, 2, 3):
        up = (shift_z(up[0], 1), shift_z(up[1], 1))
        down = (shift_z(down[0], -1), shift_z(down[1], -1))
        chunks[8 - step], chunks[step] = up, down
    chunks[4] = (shift_z(up[0], 1), shift_z(down[1], -1))
    first = sum_core(project([chunks[k] for k in (6, 7, 0, 1, 2)]))
    near = swap_y(first[:, 16:32], 1)
    second = project([chunks[k] for k in (3, 4, 5)])
    near, second = tie(near, second)
    second = sum_core(second)

    def sum_y(terms, near):
        return add(
            terms[:, :16], near, swap_y(terms[:, 32:48], 2), swap_y(terms[:, 48:64], 3)
        ).astype(BF)

    terms = jnp.concatenate(
        [sum_y(first, near), sum_y(second, swap_y(second[:, 16:32], 1))], axis=0
    )
    own_rows = add(
        terms[:, :8, :width],
        swap_x(terms[:, :8, width:], 1),
        swap_x(terms[:, 8:, :width], 2),
        swap_x(terms[:, 8:, width:], 3),
    ).reshape(rows, width)
    own_rows = lax.dynamic_slice(
        jnp.concatenate([own_rows, own_rows], axis=0), ((10 - z) % 8 * 8, 0), (rows, width)
    )
    return (values + own_rows).astype(BF)


def solution(mesh):
    return jax.shard_map(
        local,
        mesh=mesh,
        in_specs=(
            P("ffn", "hid"),
            P("ffn"),
            P(None, "hid"),
            P("hid", "ffn"),
            P("hid", "ffn"),
            P("ffn", "hid"),
        ),
        out_specs=P("ffn", "hid"),
        check_vma=False,
    )
```

```python
import jax
import jax.numpy as jnp
from jax import lax
from jax.sharding import PartitionSpec as P

AXES = ("hid", "ffn")
BF = jnp.bfloat16
F32 = jnp.float32


def permutation(move):
    pairs = []
    for xl in range(2):
        for z in range(8):
            for xh in range(2):
                for y in range(4):
                    for core in range(2):
                        x, yy, zz, cc = move(xh * 2 + xl, y, z, core)
                        source = (xl * 8 + z) * 16 + xh * 8 + y * 2 + core
                        target = ((x % 2) * 8 + zz) * 16 + (x // 2) * 8 + yy * 2 + cc
                        pairs.append((source, target))
    return pairs


def swap_x(value, bits):
    return lax.ppermute(value, AXES, permutation(lambda x, y, z, c: (x ^ bits, y, z, c)))


def swap_y(value, bits):
    return lax.ppermute(value, AXES, permutation(lambda x, y, z, c: (x, y ^ bits, z, c)))


def swap_core(value):
    return lax.ppermute(value, AXES, permutation(lambda x, y, z, c: (x, y, z, c ^ 1)))


def shift_z(value, step):
    return lax.ppermute(value, AXES, permutation(lambda x, y, z, c: (x, y, (z + step) % 8, c)))


def tie(*values):
    return lax.optimization_barrier(values)


def add(*terms):
    total = terms[0].astype(F32)
    for term in terms[1:]:
        total = total + term.astype(F32)
    return total


def high_low(value):
    high = value.astype(BF)
    low = (value - high.astype(F32)).astype(BF)
    return high, low


def local(tokens, lang_ids, gain_table, gate_weight, up_weight, down_weight):
    rows, width = tokens.shape
    units = gate_weight.shape[1]
    half = units // 2
    part_a = 512
    part_b = half - part_a
    hid = lax.axis_index("hid")
    x_lo, z = hid // 8, hid % 8

    def pick(weight, start, count, mine):
        low = weight[:, start : start + count]
        high = weight[:, half + start : half + start + count]
        return jnp.where((x_lo == 0) == mine, low, high)

    def both(start, count, mine):
        return jnp.concatenate(
            [pick(gate_weight, start, count, mine), pick(up_weight, start, count, mine)], axis=1
        )

    away_a = both(0, part_a, False)
    away_b = both(part_a, part_b, False)

    one_hot = (
        lang_ids[:, None] == jnp.arange(gain_table.shape[0], dtype=jnp.int32)[None, :]
    ).astype(F32)
    token_gains = jnp.dot(one_hot, gain_table, precision=lax.Precision.HIGHEST)
    values = tokens.astype(F32)
    scaled = (values * token_gains).astype(BF)
    squares = jnp.sum(values * values, axis=1, keepdims=True)
    high, low = high_low(squares)
    pad = jnp.zeros((rows, 126), BF)
    block = jnp.concatenate([scaled, high, low, pad], axis=1)
    block = lax.dynamic_slice(
        jnp.concatenate([block, block], axis=0), (z * 8, 0), block.shape
    ).reshape(8, 8, width + 128)

    from_1, from_2, from_3 = (swap_x(block, bits) for bits in (1, 2, 3))
    piece_a0 = swap_x(away_a[:64], 1)
    from_1, from_2, from_3, piece_a0, away_a, away_b = tie(
        from_1, from_2, from_3, piece_a0, away_a, away_b
    )
    block = jnp.concatenate(
        [
            jnp.concatenate([block, from_2], axis=1),
            jnp.concatenate([from_1, from_3], axis=1),
        ],
        axis=2,
    )
    from_1, from_2, from_3 = (swap_y(block, bits) for bits in (1, 2, 3))
    piece_a1 = swap_x(away_a[64:], 1)
    piece_b0 = swap_x(away_b[:96], 1)
    from_1, from_2, from_3, piece_a1, piece_b0, away_b = tie(
        from_1, from_2, from_3, piece_a1, piece_b0, away_b
    )
    block = jnp.concatenate([block, from_1, from_2, from_3], axis=1)
    from_core = swap_core(block)
    piece_b1 = swap_x(away_b[96:], 1)
    block = jnp.concatenate([block, from_core], axis=1)
    edge = width + 128
    here = block[:, :, :width].reshape(-1, width)
    there = block[:, :, edge : edge + width].reshape(-1, width)
    everything = jnp.concatenate([here, there], axis=1)
    square_sums = add(
        block[:, :, width],
        block[:, :, width + 1],
        block[:, :, edge + width],
        block[:, :, edge + width + 1],
    )

    weight_a = jnp.concatenate([both(0, part_a, True), piece_a0, piece_a1], axis=0)
    sums_a = (
        jnp.dot(everything, weight_a, preferred_element_type=F32)
        .astype(BF)
        .reshape(8, -1, 2 * part_a)
    )
    up_a = shift_z(sums_a[4], 1)
    up_a, piece_b1 = tie(up_a, piece_b1)
    weight_b = jnp.concatenate([both(part_a, part_b, True), piece_b0, piece_b1], axis=0)
    sums_b = (
        jnp.dot(everything, weight_b, preferred_element_type=F32)
        .astype(BF)
        .reshape(8, -1, 2 * part_b)
    )

    cut = 2 * part_b

    def with_squares(k, arrived=None):
        total = square_sums[k][:, None]
        if arrived is None:
            body = sums_b[k]
        else:
            body = add(sums_b[k], arrived[:, :cut]).astype(BF)
            total = total + add(arrived[:, cut : cut + 1], arrived[:, cut + 1 : cut + 2])
        high, low = high_low(total)
        return jnp.concatenate([body, high, low, jnp.zeros((body.shape[0], 126), BF)], axis=1)

    def pair(send_up, send_down):
        send_up, send_down = tie(send_up, send_down)
        return tie(shift_z(send_up, 1), shift_z(send_down, -1))

    down_b = shift_z(with_squares(4), -1)
    down_a = up_b = None
    for hop in (1, 2, 3):
        send_down = sums_a[5] if down_a is None else add(sums_a[4 + hop], down_a).astype(BF)
        up_a, down_a = pair(add(sums_a[4 - hop], up_a).astype(BF), send_down)
        if hop == 2:
            up_a, down_weight = tie(up_a, down_weight)
        up_b, down_b = pair(with_squares(4 - hop, up_b), with_squares(4 + hop, down_b))

    all_squares = square_sums[0][:, None] + add(
        up_b[:, cut : cut + 1],
        up_b[:, cut + 1 : cut + 2],
        down_b[:, cut : cut + 1],
        down_b[:, cut + 1 : cut + 2],
    )
    inverse_rms = lax.rsqrt(all_squares / (width * 16) + 1e-05)

    def activate(summed, count):
        gate = summed[:, :count] * inverse_rms
        up = summed[:, count:] * inverse_rms
        return (jax.nn.silu(gate) * up).astype(BF)

    hidden_a = activate(add(sums_a[0], up_a, down_a), part_a)
    hidden_b = activate(add(sums_b[0], up_b[:, :cut], down_b[:, :cut]), part_b)

    down_low, down_high = down_weight[:half], down_weight[half:]
    down_there = swap_x(jnp.where(x_lo == 0, down_high, down_low), 1)
    down_here = jnp.where(x_lo == 0, down_low, down_high)
    down_both = jnp.concatenate([down_here, down_there], axis=1)

    def project(chunks):
        terms = jnp.dot(
            jnp.concatenate(chunks, axis=0), down_both, preferred_element_type=F32
        )
        return terms.astype(BF).reshape(len(chunks), 128, 2 * width)

    def sum_core(terms):
        return add(terms[:, :64], swap_core(terms[:, 64:])).astype(BF)

    up = down = jnp.concatenate([hidden_a, hidden_b], axis=1)
    chunks = {0: up}
    for step in (1, 2, 3):
        up, down = tie(up, down)
        up, down = shift_z(up, 1), shift_z(down, -1)
        chunks[8 - step], chunks[step] = up, down
    up, down = tie(up[:, :512], down[:, 512:])
    chunks[4] = jnp.concatenate([shift_z(up, 1), shift_z(down, -1)], axis=1)
    first = sum_core(project([chunks[k] for k in (6, 7, 0, 1, 2)]))
    near = swap_y(first[:, 16:32], 1)
    second = project([chunks[k] for k in (3, 4, 5)])
    near, second = tie(near, second)
    second = sum_core(second)

    def sum_y(terms, near):
        return add(
            terms[:, :16], near, swap_y(terms[:, 32:48], 2), swap_y(terms[:, 48:64], 3)
        ).astype(BF)

    terms = jnp.concatenate(
        [sum_y(first, near), sum_y(second, swap_y(second[:, 16:32], 1))], axis=0
    )
    own_rows = add(
        terms[:, :8, :width],
        swap_x(terms[:, :8, width:], 1),
        swap_x(terms[:, 8:, :width], 2),
        swap_x(terms[:, 8:, width:], 3),
    ).reshape(rows, width)
    own_rows = lax.dynamic_slice(
        jnp.concatenate([own_rows, own_rows], axis=0), ((10 - z) % 8 * 8, 0), (rows, width)
    )
    return (values + own_rows).astype(BF)


def solution(mesh):
    return jax.shard_map(
        local,
        mesh=mesh,
        in_specs=(
            P("ffn", "hid"),
            P("ffn"),
            P(None, "hid"),
            P("hid", "ffn"),
            P("hid", "ffn"),
            P("ffn", "hid"),
        ),
        out_specs=P("ffn", "hid"),
        check_vma=False,
    )
```

```python
import jax
import jax.numpy as jnp
from jax import lax
from jax.sharding import PartitionSpec as P

AXES = ("hid", "ffn")
BF = jnp.bfloat16
F32 = jnp.float32


def permutation(move):
    pairs = []
    for xl in range(2):
        for z in range(8):
            for xh in range(2):
                for y in range(4):
                    for core in range(2):
                        x, yy, zz, cc = move(xh * 2 + xl, y, z, core)
                        source = (xl * 8 + z) * 16 + xh * 8 + y * 2 + core
                        target = ((x % 2) * 8 + zz) * 16 + (x // 2) * 8 + yy * 2 + cc
                        pairs.append((source, target))
    return pairs


def swap_x(value, bits):
    return lax.ppermute(value, AXES, permutation(lambda x, y, z, c: (x ^ bits, y, z, c)))


def swap_y(value, bits):
    return lax.ppermute(value, AXES, permutation(lambda x, y, z, c: (x, y ^ bits, z, c)))


def swap_core(value):
    return lax.ppermute(value, AXES, permutation(lambda x, y, z, c: (x, y, z, c ^ 1)))


def shift_z(value, step):
    return lax.ppermute(value, AXES, permutation(lambda x, y, z, c: (x, y, (z + step) % 8, c)))


def tie(*values):
    return lax.optimization_barrier(values)


def add(*terms):
    total = terms[0].astype(F32)
    for term in terms[1:]:
        total = total + term.astype(F32)
    return total


def high_low(value):
    high = value.astype(BF)
    low = (value - high.astype(F32)).astype(BF)
    return high, low


def local(tokens, lang_ids, gain_table, gate_weight, up_weight, down_weight):
    rows, width = tokens.shape
    units = gate_weight.shape[1]
    half = units // 2
    part_a = 512
    part_b = half - part_a
    hid = lax.axis_index("hid")
    x_lo, z = hid // 8, hid % 8

    def pick(weight, start, count, mine):
        low = weight[:, start : start + count]
        high = weight[:, half + start : half + start + count]
        return jnp.where((x_lo == 0) == mine, low, high)

    def both(start, count, mine):
        return jnp.concatenate(
            [pick(gate_weight, start, count, mine), pick(up_weight, start, count, mine)], axis=1
        )

    away_a = both(0, part_a, False)
    away_b = both(part_a, part_b, False)

    one_hot = (
        lang_ids[:, None] == jnp.arange(gain_table.shape[0], dtype=jnp.int32)[None, :]
    ).astype(F32)
    token_gains = jnp.dot(one_hot, gain_table, precision=lax.Precision.HIGHEST)
    values = tokens.astype(F32)
    scaled = (values * token_gains).astype(BF)
    squares = jnp.sum(values * values, axis=1, keepdims=True)
    high, low = high_low(squares)
    pad = jnp.zeros((rows, 126), BF)
    block = jnp.concatenate([scaled, high, low, pad], axis=1)
    block = lax.dynamic_slice(
        jnp.concatenate([block, block], axis=0), (z * 8, 0), block.shape
    ).reshape(8, 8, width + 128)

    from_1, from_2, from_3 = (swap_x(block, bits) for bits in (1, 2, 3))
    piece_a0 = swap_x(away_a[:64], 1)
    from_1, from_2, from_3, piece_a0, away_a, away_b = tie(
        from_1, from_2, from_3, piece_a0, away_a, away_b
    )
    block = jnp.concatenate(
        [
            jnp.concatenate([block, from_2], axis=1),
            jnp.concatenate([from_1, from_3], axis=1),
        ],
        axis=2,
    )
    from_1, from_2, from_3 = (swap_y(block, bits) for bits in (1, 2, 3))
    piece_a1 = swap_x(away_a[64:], 1)
    piece_b0 = swap_x(away_b[:96], 1)
    from_1, from_2, from_3, piece_a1, piece_b0, away_b = tie(
        from_1, from_2, from_3, piece_a1, piece_b0, away_b
    )
    block = jnp.concatenate([block, from_1, from_2, from_3], axis=1)
    from_core = swap_core(block)
    piece_b1 = swap_x(away_b[96:], 1)
    block = jnp.concatenate([block, from_core], axis=1)
    edge = width + 128
    here = block[:, :, :width].reshape(-1, width)
    there = block[:, :, edge : edge + width].reshape(-1, width)
    everything = jnp.concatenate([here, there], axis=1)
    square_sums = add(
        block[:, :, width],
        block[:, :, width + 1],
        block[:, :, edge + width],
        block[:, :, edge + width + 1],
    )

    weight_a = jnp.concatenate([both(0, part_a, True), piece_a0, piece_a1], axis=0)
    sums_a = (
        jnp.dot(everything, weight_a, preferred_element_type=F32)
        .astype(BF)
        .reshape(8, -1, 2 * part_a)
    )
    up_a = shift_z(sums_a[4], 1)
    up_a, piece_b1 = tie(up_a, piece_b1)
    weight_b = jnp.concatenate([both(part_a, part_b, True), piece_b0, piece_b1], axis=0)
    sums_b = (
        jnp.dot(everything, weight_b, preferred_element_type=F32)
        .astype(BF)
        .reshape(8, -1, 2 * part_b)
    )

    cut = 2 * part_b

    def with_squares(k, arrived=None):
        total = square_sums[k][:, None]
        if arrived is None:
            body = sums_b[k]
        else:
            body = add(sums_b[k], arrived[:, :cut]).astype(BF)
            total = total + add(arrived[:, cut : cut + 1], arrived[:, cut + 1 : cut + 2])
        high, low = high_low(total)
        return jnp.concatenate([body, high, low, jnp.zeros((body.shape[0], 126), BF)], axis=1)

    def pair(send_up, send_down):
        send_up, send_down = tie(send_up, send_down)
        return tie(shift_z(send_up, 1), shift_z(send_down, -1))

    down_b = shift_z(with_squares(4), -1)
    down_a = up_b = None
    for hop in (1, 2, 3):
        send_down = sums_a[5] if down_a is None else add(sums_a[4 + hop], down_a).astype(BF)
        up_a, down_a = pair(add(sums_a[4 - hop], up_a).astype(BF), send_down)
        if hop == 2:
            up_a, down_weight = tie(up_a, down_weight)
        up_b, down_b = pair(with_squares(4 - hop, up_b), with_squares(4 + hop, down_b))

    all_squares = square_sums[0][:, None] + add(
        up_b[:, cut : cut + 1],
        up_b[:, cut + 1 : cut + 2],
        down_b[:, cut : cut + 1],
        down_b[:, cut + 1 : cut + 2],
    )
    inverse_rms = lax.rsqrt(all_squares / (width * 16) + 1e-05)

    def activate(summed, count):
        gate = summed[:, :count] * inverse_rms
        up = summed[:, count:] * inverse_rms
        return (jax.nn.silu(gate) * up).astype(BF)

    hidden_a = activate(add(sums_a[0], up_a, down_a), part_a)
    hidden_b = activate(add(sums_b[0], up_b[:, :cut], down_b[:, :cut]), part_b)

    down_low, down_high = down_weight[:half], down_weight[half:]
    down_there = swap_x(jnp.where(x_lo == 0, down_high, down_low), 1)
    down_here = jnp.where(x_lo == 0, down_low, down_high)
    down_both = jnp.concatenate([down_here, down_there], axis=1)

    def project(chunks):
        terms = jnp.dot(
            jnp.concatenate(chunks, axis=0), down_both, preferred_element_type=F32
        )
        return terms.astype(BF).reshape(len(chunks), 128, 2 * width)

    def sum_core(terms):
        return add(terms[:, :64], swap_core(terms[:, 64:])).astype(BF)

    up = down = jnp.concatenate([hidden_a, hidden_b], axis=1)
    chunks = {0: up}
    for step in (1, 2, 3):
        if step == 2:
            up, down_both = tie(up, down_both)
        up, down = tie(up, down)
        up, down = shift_z(up, 1), shift_z(down, -1)
        chunks[8 - step], chunks[step] = up, down
    up, down = tie(up[:, :512], down[:, 512:])
    chunks[4] = jnp.concatenate([shift_z(up, 1), shift_z(down, -1)], axis=1)
    first = sum_core(project([chunks[k] for k in (6, 7, 0, 1, 2)]))
    near = swap_y(first[:, 16:32], 1)
    second = project([chunks[k] for k in (3, 4, 5)])
    near, second = tie(near, second)
    second = sum_core(second)

    def sum_y(terms, near):
        return add(
            terms[:, :16], near, swap_y(terms[:, 32:48], 2), swap_y(terms[:, 48:64], 3)
        ).astype(BF)

    terms = jnp.concatenate(
        [sum_y(first, near), sum_y(second, swap_y(second[:, 16:32], 1))], axis=0
    )
    own_rows = add(
        terms[:, :8, :width],
        swap_x(terms[:, :8, width:], 1),
        swap_x(terms[:, 8:, :width], 2),
        swap_x(terms[:, 8:, width:], 3),
    ).reshape(rows, width)
    own_rows = lax.dynamic_slice(
        jnp.concatenate([own_rows, own_rows], axis=0), ((10 - z) % 8 * 8, 0), (rows, width)
    )
    return (values + own_rows).astype(BF)


def solution(mesh):
    return jax.shard_map(
        local,
        mesh=mesh,
        in_specs=(
            P("ffn", "hid"),
            P("ffn"),
            P(None, "hid"),
            P("hid", "ffn"),
            P("hid", "ffn"),
            P("ffn", "hid"),
        ),
        out_specs=P("ffn", "hid"),
        check_vma=False,
    )
```
